128 devices in a mesh: bins: 8 (over y, core), space: 16 (over z, x).
Axes of the slice: x: 4, y: 4, z: 4, core: 2. Of those that a mesh axis runs over, the one named last changes fastest.
Arguments:
- spectra: float32 [1152, 1024, 128], P('bins', 'space'), may hold values from 0.05 to 2
- land_mask: int32 [1024, 128], P('space'), may hold values 0 or 1
- growth: float32 [1152], replicated, may hold values from 0.1 to 1
- band_weight: float32 [1152], replicated, may hold values from 0.00043402778 to 0.0034722222
- kernel_gain: bfloat16 [1152, 1152], replicated, may hold values from -0.1875 to 0.1875
- kernel_loss: bfloat16 [1152, 1152], replicated, may hold values from -0.1875 to 0.1875
Outputs:
- updated: float32 [1152, 1024, 128], P('bins', 'space')
The draws below stay inside these ranges and needn't reach their ends.
All inputs are finite; a program needn't handle non-finite values. No bound on the sum of `land_mask` on one device may be relied on, other than what follows from the above.
Results may differ from the reference program's by a relative error of at most 0.00056.
Values sent between devices are 32-bit elements; how exact they have to be, the bound alone decides.
A program may use at most 64 MiB of HBM per device.

```python
import math
import jax
import jax.numpy as jnp
from jax import lax

NF = 32
ND = 36
NB = 1152
CX = 64
NY = 128
SUBSTEPS = 4
NX = 1024
N_SPACE = 16


def plant(array, key, low, largest):
    shape = array.shape
    place = [jax.random.randint(jax.random.fold_in(key, axis), (), 0, shape[axis]) for axis in range(len(shape))]
    array = array.at[tuple(place)].set(low)
    longest = shape.index(max(shape))
    place[longest] = (place[longest] + 1) % shape[longest]
    return array.at[tuple(place)].set(largest)


def steps_of(stream_key, extent, cuts, smallest, high):
    def one(axis_at, blocks):
        steps = jax.random.uniform(jax.random.fold_in(jax.random.fold_in(stream_key, 6), axis_at), (blocks,), jnp.float32, smallest / len(cuts), high / len(cuts))
        return jnp.repeat(jnp.exp(steps), extent[axis_at] // blocks).reshape((-1,) + (1,) * (len(extent) - axis_at - 1))

    level = one(*cuts[0])
    for cut in cuts[1:]:
        level = level * one(*cut)
    return level


def normal_values(stream_key, dims, spread, limit, held_as=jnp.bfloat16):
    entries = jax.random.normal(stream_key, dims, jnp.float32) * spread
    return jnp.minimum(jnp.maximum(entries, -limit), limit).astype(held_as)


def setup_inputs(seed: int = 0) -> dict:
    splits = jax.random.split(jax.random.key(seed), 7)
    return {
        "spectra": jnp.clip(jnp.exp(math.log(2.0) - 3.6888794 * jax.random.uniform(splits[0], (NB, NX, NY), jnp.float32) ** steps_of(splits[0], (NB, NX, NY), ((0, 8), (1, 16)), -0.2, 0.2)), 0.05, 2.0),
        "land_mask": plant((jax.random.randint(splits[1], (NX, NY), 0, 4) < 3).astype(jnp.int32), jax.random.fold_in(splits[1], 1), 0, 1),
        "growth": jnp.clip(jnp.exp(jax.random.uniform(splits[2], (NB,), jnp.float32, math.log(0.1), math.log(1.0))), 0.1, 1.0),
        "band_weight": jnp.clip(jnp.exp(jax.random.uniform(splits[3], (NB,), jnp.float32, math.log(0.00043402778), math.log(0.0034722222))), 0.00043402778, 0.0034722222),
        "kernel_gain": normal_values(splits[4], (NB, NB), NB ** -0.5, 0.1875),
        "kernel_loss": normal_values(splits[5], (NB, NB), NB ** -0.5, 0.1875),
    }


def courants():
    index = jnp.arange(NB, dtype=jnp.int32)
    freq = (index // ND).astype(jnp.float32)
    direc = (index % ND).astype(jnp.float32)
    group = 1.0 / (1.0 + 2.3 * freq / max(NF - 1, 1))
    theta = 2.0 * math.pi * (direc + 0.5) / ND
    return 0.9 * group * jnp.cos(theta), 0.9 * group * jnp.sin(theta)


def upwind(field, speed, axis):
    plus = jnp.maximum(speed, 0.0)
    minus = jnp.maximum(-speed, 0.0)
    count = field.shape[axis]
    widths = [(0, 0)] * field.ndim
    widths[axis] = (1, 1)
    padded = jnp.pad(field, widths)
    lower = lax.slice_in_dim(padded, 0, count, axis=axis)
    upper = lax.slice_in_dim(padded, 2, count + 2, axis=axis)
    return field - plus * (field - lower) - minus * (field - upper)


def sources(block, growth, band_weight, kernel_gain, kernel_loss):
    state = block.astype(jnp.bfloat16)
    square = (block * block).astype(jnp.bfloat16)
    gain = jnp.dot(kernel_gain, state, preferred_element_type=jnp.float32)
    loss = jnp.dot(kernel_loss, square, preferred_element_type=jnp.float32)
    energy = jnp.sum(band_weight[:, None] * block, axis=0)
    return (block + 0.25 * (growth[:, None] * block + block * gain - loss)) / (1.0 + 0.5 * energy)


def reference(spectra, land_mask, growth, band_weight, kernel_gain, kernel_loss):
    speed_x, speed_y = courants()
    sea = land_mask.astype(jnp.float32)
    field = spectra
    for step in range(SUBSTEPS):
        field = upwind(field, speed_x[:, None, None], 1)
        field = upwind(field, speed_y[:, None, None], 2)
        field = sea[None] * field
    blocks = field.reshape(NB, N_SPACE, CX * NY).transpose(1, 0, 2)
    result = lax.map(lambda block: sources(block, growth, band_weight, kernel_gain, kernel_loss), blocks)
    result = result.transpose(1, 0, 2).reshape(NB, NX, NY)
    return sea[None] * result
```

```python
import functools
import math

import jax
import jax.numpy as jnp
import numpy as np
from jax import lax
from jax.experimental import pallas as pl
from jax.experimental.pallas import tpu as pltpu
from jax.sharding import PartitionSpec as P

NF = 32
ND = 36
SUBSTEPS = 4
PEERS = 8
SLABS = 16
LB = 144
NB = 1152
ROWS = 64
COLS = 128
PAD = ROWS + 16
ROUNDS = 8
MESH = pl.DeviceIdType.MESH


def device_of(slot):
    return (slot % 4) * 2 + slot // 4


def slot_of(device):
    return device // 2 + 4 * lax.rem(device, 2)


def kernel(x, mask, cosv, sinv, grow, band, kg, kl, out,
           fin, seab, mlo, mhi, sent, got, fresh, back, outv, kgv, klv, growb, bandb, state, square,
           load_sem, halo_send, halo_recv, own_sem, fs, fr, bs, br, out_sem):
    me = lax.axis_index("bins")
    space = lax.axis_index("space")
    up = lax.rem(space + 1, SLABS)
    down = lax.rem(space + SLABS - 1, SLABS)

    barrier = pltpu.get_barrier_semaphore()
    for i in range(1, PEERS):
        pl.semaphore_signal(barrier, inc=1, device_id=(lax.rem(me + i, PEERS), space), device_id_type=MESH)
    for other in (up, down):
        pl.semaphore_signal(barrier, inc=1, device_id=(me, other), device_id_type=MESH)

    def load(q):
        return pltpu.make_async_copy(x.at[:, pl.ds(8 * q, 8), :], fin.at[:, pl.ds(8 * q + 8, 8), :], load_sem.at[q])

    for q in (1, 2, 3, 4, 5, 6, 0, 7):
        load(q).start()
    weights = [pltpu.make_async_copy(kg, kgv, load_sem.at[8]), pltpu.make_async_copy(kl, klv, load_sem.at[9])]

    for q in range(ROWS // 8):
        sea = mask[8 * q:8 * q + 8, :].astype(jnp.float32)
        for i in range(8):
            seab[8 + 8 * q + i] = jnp.broadcast_to(sea[i:i + 1, :], (8, COLS))

    halos = [
        pltpu.make_async_remote_copy(x.at[:, pl.ds(56, 8), :], fin.at[:, pl.ds(0, 8), :], halo_send.at[0], halo_recv.at[0],
                                     device_id=(me, up), device_id_type=MESH),
        pltpu.make_async_remote_copy(x.at[:, pl.ds(0, 8), :], fin.at[:, pl.ds(72, 8), :], halo_send.at[1], halo_recv.at[1],
                                     device_id=(me, down), device_id_type=MESH),
        pltpu.make_async_remote_copy(mask.at[pl.ds(56, 8), :], mlo, halo_send.at[2], halo_recv.at[2],
                                     device_id=(me, up), device_id_type=MESH),
        pltpu.make_async_remote_copy(mask.at[pl.ds(0, 8), :], mhi, halo_send.at[3], halo_recv.at[3],
                                     device_id=(me, down), device_id_type=MESH),
    ]
    inside_lo = (space > 0).astype(jnp.float32)
    inside_hi = (space < SLABS - 1).astype(jnp.float32)
    flat = fin.reshape(LB * PAD, COLS)
    lane = lax.broadcasted_iota(jnp.int32, (8, COLS), 1)
    sub = lax.broadcasted_iota(jnp.int32, (8, COLS), 0)

    def propagate(g):
        def tile(t, carry):
            b0 = pl.multiple_of(t * 8, 8)
            rows = [flat[pl.ds(b0 * PAD + 16 * g + 4 + i, 8, stride=PAD), :] for i in range(24)]
            if g == 0:
                rows = [r * inside_lo for r in rows[:4]] + rows[4:]
            if g == 3:
                rows = rows[:20] + [r * inside_hi for r in rows[20:]]
            field = jnp.stack(rows)
            b = sub + b0
            one = lambda c: c.astype(jnp.float32)
            freq = (4 * me).astype(jnp.float32) + one(b >= ND) + one(b >= 2 * ND) + one(b >= 3 * ND)
            group = 0.9 / (1.0 + 2.3 * freq / max(NF - 1, 1))
            cx = group * cosv[pl.ds(b0, 8), :]
            cy = group * sinv[pl.ds(b0, 8), :]
            right, ahead = cx > 0.0, cy > 0.0
            ax, ay = jnp.abs(cx), jnp.abs(cy)
            stay = 1.0 - ay
            move = jnp.where((ahead & (lane == 0)) | (~ahead & (lane == COLS - 1)), 0.0, ay)
            for step in range(SUBSTEPS):
                n = field.shape[0] - 2
                mid = field[1:-1]
                near = jnp.where(right[None], field[:-2], field[2:])
                mid = mid + ax[None] * (near - mid)
                near = jnp.stack([jnp.where(ahead, pltpu.roll(mid[i], 1, 1), pltpu.roll(mid[i], COLS - 1, 1)) for i in range(n)])
                field = (stay[None] * mid + move[None] * near) * seab[pl.ds(16 * g + 5 + step, n)]
            sent[pl.ds(16 * g, 16), pl.ds(b0, 8), :] = field
            return carry
        lax.fori_loop(0, LB // 8, tile, 0)

    def forward(j, d):
        row = 8 * j + slot_of(d)
        return pltpu.make_async_remote_copy(
            sent.at[row], got.at[j, pl.ds(me * LB, LB), :], fs.at[j, d], fr.at[j, me],
            device_id=(d, space), device_id_type=MESH)

    def arrival(j, d):
        return pltpu.make_async_remote_copy(
            sent.at[0], got.at[j, pl.ds(d * LB, LB), :], fs.at[j, d], fr.at[j, d],
            device_id=(d, space), device_id_type=MESH)

    def own(j):
        return pltpu.make_async_copy(sent.at[8 * j + slot_of(me)], got.at[j, pl.ds(me * LB, LB), :], own_sem.at[0, j])

    def give(j, d):
        return pltpu.make_async_remote_copy(
            fresh.at[j, pl.ds(d * LB, LB), :], back.at[pl.ds((8 * j + slot_of(me)) * LB, LB), :], bs.at[j, d], br.at[j, me],
            device_id=(d, space), device_id_type=MESH)

    def returned(j, d):
        return pltpu.make_async_remote_copy(
            fresh.at[j, pl.ds(d * LB, LB), :], back.at[pl.ds((8 * j + slot_of(d)) * LB, LB), :], bs.at[j, d], br.at[j, d],
            device_id=(d, space), device_id_type=MESH)

    def keep(j):
        return pltpu.make_async_copy(
            fresh.at[j, pl.ds(me * LB, LB), :], back.at[pl.ds((8 * j + slot_of(me)) * LB, LB), :], own_sem.at[1, j])

    def others(body):
        def step(i, carry):
            body(lax.rem(me + i, PEERS))
            return carry
        lax.fori_loop(1, PEERS, step, 0)

    ready = set()
    first = True
    for g in (1, 2, 0, 3):
        for q in range(max(2 * g - 1, 0), min(2 * g + 3, 8)):
            if q not in ready:
                load(q).wait()
                ready.add(q)
        if g == 0:
            for h in halos:
                h.wait_recv()
            for q, (ref, inside) in ((0, (mlo, inside_lo)), (72, (mhi, inside_hi))):
                sea = ref[...].astype(jnp.float32) * inside
                for i in range(8):
                    seab[q + i] = jnp.broadcast_to(sea[i:i + 1, :], (8, COLS))
        propagate(g)
        if first:
            pl.semaphore_wait(barrier, PEERS + 1)
            for h in halos:
                h.start()
            first = False
        for j in (2 * g, 2 * g + 1):
            others(lambda d: forward(j, d).start())
            own(j).start()
        if g == 2:
            for w in weights:
                w.start()
            for i in range(NB // COLS):
                at = pl.ds(i * COLS, COLS)
                growb[at, :] = jnp.transpose(jnp.broadcast_to(0.25 * grow[i:i + 1, :] + 1.0, (COLS, COLS)))
                bandb[at, :] = jnp.transpose(jnp.broadcast_to(band[i:i + 1, :], (COLS, COLS)))
    for w in weights:
        w.wait()

    order = (2, 3, 4, 5, 0, 1, 6, 7)

    def sources(j):
        others(lambda d: arrival(j, d).wait_recv())
        own(j).wait()

        def prepare(i, total):
            at = pl.ds(pl.multiple_of(i * LB, LB), LB)
            field = got[j, at, :]
            state[at, :] = field.astype(jnp.bfloat16)
            square[at, :] = (field * field).astype(jnp.bfloat16)
            return total + jnp.sum((bandb[at, :] * field).reshape(LB // 8, 8, COLS), axis=0)
        energy = jnp.sum(lax.fori_loop(0, PEERS, prepare, jnp.zeros((8, COLS), jnp.float32)), axis=0, keepdims=True)
        damp = 1.0 / (1.0 + 0.5 * energy)

        def owner(i, carry):
            d = lax.rem(me + i, PEERS)
            at = pl.ds(pl.multiple_of(d * LB, LB), LB)
            gain = jnp.dot(kgv[at, :], state[...], preferred_element_type=jnp.float32)
            loss = jnp.dot(klv[at, :], square[...], preferred_element_type=jnp.float32)
            field = got[j, at, :]
            fresh[j, at, :] = (field * (growb[at, :] + 0.25 * gain) - 0.25 * loss) * damp

            @pl.when(i < PEERS)
            def _():
                give(j, d).start()
            return carry
        lax.fori_loop(1, PEERS + 1, owner, 0)
        keep(j).start()

    for j in order:
        sources(j)

    def save(j):
        return pltpu.make_async_copy(outv.at[:, pl.ds(8 * j, 8), :], out.at[:, pl.ds(8 * j, 8), :], out_sem.at[j])

    for j in order:
        others(lambda d: returned(j, d).wait_recv())
        keep(j).wait()
        sea = mask[8 * j:8 * j + 8, :].astype(jnp.float32)

        def turn(b, carry):
            outv[b, pl.ds(8 * j, 8), :] = back[pl.ds(8 * j * LB + b, 8, stride=LB), :] * sea
            return carry
        lax.fori_loop(0, LB, turn, 0, unroll=8)
        save(j).start()

    for h in halos:
        h.wait_send()
    for j in order:
        others(lambda d: forward(j, d).wait_send())
        others(lambda d: give(j, d).wait_send())
    for j in order:
        save(j).wait()


def local(spectra, land_mask, growth, band_weight, kernel_gain, kernel_loss):
    theta = 2.0 * math.pi * (np.arange(LB) % ND + 0.5) / ND
    wide = lambda v: jnp.asarray(np.repeat(v.astype(np.float32)[:, None], COLS, 1))
    vmem = pl.BlockSpec(memory_space=pltpu.VMEM)
    anym = pl.BlockSpec(memory_space=pl.ANY)
    f32, bf16 = jnp.float32, jnp.bfloat16
    dma = pltpu.SemaphoreType.DMA
    return pl.pallas_call(
        kernel,
        out_shape=jax.ShapeDtypeStruct((LB, ROWS, COLS), f32),
        in_specs=[anym, vmem, vmem, vmem, vmem, vmem, anym, anym],
        out_specs=anym,
        scratch_shapes=[
            pltpu.VMEM((LB, PAD, COLS), f32),
            pltpu.VMEM((PAD, 8, COLS), f32),
            pltpu.VMEM((8, COLS), jnp.int32),
            pltpu.VMEM((8, COLS), jnp.int32),
            pltpu.VMEM((ROWS, LB, COLS), f32),
            pltpu.VMEM((ROUNDS, NB, COLS), f32),
            pltpu.VMEM((ROUNDS, NB, COLS), f32),
            pltpu.VMEM((ROWS * LB, COLS), f32),
            pltpu.VMEM((LB, ROWS, COLS), f32),
            pltpu.VMEM((NB, NB), bf16),
            pltpu.VMEM((NB, NB), bf16),
            pltpu.VMEM((NB, COLS), f32),
            pltpu.VMEM((NB, COLS), f32),
            pltpu.VMEM((NB, COLS), bf16),
            pltpu.VMEM((NB, COLS), bf16),
            dma((10,)), dma((4,)), dma((4,)), dma((2, ROUNDS)),
            dma((ROUNDS, PEERS)), dma((ROUNDS, PEERS)), dma((ROUNDS, PEERS)), dma((ROUNDS, PEERS)),
            dma((ROUNDS,)),
        ],
        compiler_params=pltpu.CompilerParams(collective_id=0, has_side_effects=True, vmem_limit_bytes=56 * 2**20),
    )(spectra, land_mask, wide(np.cos(theta)), wide(np.sin(theta)),
      growth.reshape(NB // COLS, COLS), band_weight.reshape(NB // COLS, COLS), kernel_gain, kernel_loss)


def solution(mesh):
    in_specs = (P("bins", "space", None), P("space", None), P(), P(), P(), P())
    out_specs = P("bins", "space", None)
    return jax.shard_map(local, mesh=mesh, in_specs=in_specs, out_specs=out_specs, check_vma=False)
```

```python
import functools
import math

import jax
import jax.numpy as jnp
import numpy as np
from jax import lax
from jax.experimental import pallas as pl
from jax.experimental.pallas import tpu as pltpu
from jax.sharding import PartitionSpec as P

NF = 32
ND = 36
SUBSTEPS = 4
PEERS = 8
SLABS = 16
LB = 144
NB = 1152
ROWS = 64
COLS = 128
PAD = ROWS + 16
ROUNDS = 8
MESH = pl.DeviceIdType.MESH


def device_of(slot):
    return (slot % 4) * 2 + slot // 4


def slot_of(device):
    return device // 2 + 4 * lax.rem(device, 2)


def advance(field, b0, me, cosv, sinv, lane, sub, sea):
    b = sub + b0
    one = lambda c: c.astype(jnp.float32)
    freq = (4 * me).astype(jnp.float32) + one(b >= ND) + one(b >= 2 * ND) + one(b >= 3 * ND)
    group = 0.9 / (1.0 + 2.3 * freq / max(NF - 1, 1))
    cx = group * cosv[pl.ds(b0, 8), :]
    cy = group * sinv[pl.ds(b0, 8), :]
    right, ahead = cx > 0.0, cy > 0.0
    ax, ay = jnp.abs(cx), jnp.abs(cy)
    stay = 1.0 - ay
    move = jnp.where((ahead & (lane == 0)) | (~ahead & (lane == COLS - 1)), 0.0, ay)
    for step in range(SUBSTEPS):
        n = field.shape[0] - 2
        mid = field[1:-1]
        near = jnp.where(right[None], field[:-2], field[2:])
        mid = mid + ax[None] * (near - mid)
        near = jnp.stack([jnp.where(ahead, pltpu.roll(mid[i], 1, 1), pltpu.roll(mid[i], COLS - 1, 1)) for i in range(n)])
        field = (stay[None] * mid + move[None] * near) * sea(step, n)
    return field


def whole_kernel(x, mask, cosv, sinv, grow, band, kg, kl, out,
           fin, seab, mlo, mhi, sent, got, fresh, back, outv, kgv, klv, growb, bandb, state, square,
           load_sem, halo_send, halo_recv, own_sem, fs, fr, bs, br, out_sem):
    me = lax.axis_index("bins")
    space = lax.axis_index("space")
    up = lax.rem(space + 1, SLABS)
    down = lax.rem(space + SLABS - 1, SLABS)

    barrier = pltpu.get_barrier_semaphore()
    for i in range(1, PEERS):
        pl.semaphore_signal(barrier, inc=1, device_id=(lax.rem(me + i, PEERS), space), device_id_type=MESH)
    for other in (up, down):
        pl.semaphore_signal(barrier, inc=1, device_id=(me, other), device_id_type=MESH)

    def load(q):
        return pltpu.make_async_copy(x.at[:, pl.ds(8 * q, 8), :], fin.at[:, pl.ds(8 * q + 8, 8), :], load_sem.at[q])

    for q in (1, 2, 3, 4, 5, 6, 0, 7):
        load(q).start()
    weights = [pltpu.make_async_copy(kg, kgv, load_sem.at[8]), pltpu.make_async_copy(kl, klv, load_sem.at[9])]

    for q in range(ROWS // 8):
        sea = mask[8 * q:8 * q + 8, :].astype(jnp.float32)
        for i in range(8):
            seab[8 + 8 * q + i] = jnp.broadcast_to(sea[i:i + 1, :], (8, COLS))

    halos = [
        pltpu.make_async_remote_copy(x.at[:, pl.ds(56, 8), :], fin.at[:, pl.ds(0, 8), :], halo_send.at[0], halo_recv.at[0],
                                     device_id=(me, up), device_id_type=MESH),
        pltpu.make_async_remote_copy(x.at[:, pl.ds(0, 8), :], fin.at[:, pl.ds(72, 8), :], halo_send.at[1], halo_recv.at[1],
                                     device_id=(me, down), device_id_type=MESH),
        pltpu.make_async_remote_copy(mask.at[pl.ds(56, 8), :], mlo, halo_send.at[2], halo_recv.at[2],
                                     device_id=(me, up), device_id_type=MESH),
        pltpu.make_async_remote_copy(mask.at[pl.ds(0, 8), :], mhi, halo_send.at[3], halo_recv.at[3],
                                     device_id=(me, down), device_id_type=MESH),
    ]
    inside_lo = (space > 0).astype(jnp.float32)
    inside_hi = (space < SLABS - 1).astype(jnp.float32)
    flat = fin.reshape(LB * PAD, COLS)
    lane = lax.broadcasted_iota(jnp.int32, (8, COLS), 1)
    sub = lax.broadcasted_iota(jnp.int32, (8, COLS), 0)

    def propagate(g):
        def tile(t, carry):
            b0 = pl.multiple_of(t * 8, 8)
            rows = [flat[pl.ds(b0 * PAD + 16 * g + 4 + i, 8, stride=PAD), :] for i in range(24)]
            if g == 0:
                rows = [r * inside_lo for r in rows[:4]] + rows[4:]
            if g == 3:
                rows = rows[:20] + [r * inside_hi for r in rows[20:]]
            field = jnp.stack(rows)
            field = advance(field, b0, me, cosv, sinv, lane, sub, lambda step, n: seab[pl.ds(16 * g + 5 + step, n)])
            sent[pl.ds(16 * g, 16), pl.ds(b0, 8), :] = field
            return carry
        lax.fori_loop(0, LB // 8, tile, 0, unroll=2)

    def forward(j, d):
        row = 8 * j + slot_of(d)
        return pltpu.make_async_remote_copy(
            sent.at[row], got.at[j, pl.ds(me * LB, LB), :], fs.at[j, d], fr.at[j, me],
            device_id=(d, space), device_id_type=MESH)

    def arrival(j, d):
        return pltpu.make_async_remote_copy(
            sent.at[0], got.at[j, pl.ds(d * LB, LB), :], fs.at[j, d], fr.at[j, d],
            device_id=(d, space), device_id_type=MESH)

    def own(j):
        return pltpu.make_async_copy(sent.at[8 * j + slot_of(me)], got.at[j, pl.ds(me * LB, LB), :], own_sem.at[0, j])

    def give(j, d):
        return pltpu.make_async_remote_copy(
            fresh.at[j, pl.ds(d * LB, LB), :], back.at[pl.ds((8 * j + slot_of(me)) * LB, LB), :], bs.at[j, d], br.at[j, me],
            device_id=(d, space), device_id_type=MESH)

    def returned(j, d):
        return pltpu.make_async_remote_copy(
            fresh.at[j, pl.ds(d * LB, LB), :], back.at[pl.ds((8 * j + slot_of(d)) * LB, LB), :], bs.at[j, d], br.at[j, d],
            device_id=(d, space), device_id_type=MESH)

    def keep(j):
        return pltpu.make_async_copy(
            fresh.at[j, pl.ds(me * LB, LB), :], back.at[pl.ds((8 * j + slot_of(me)) * LB, LB), :], own_sem.at[1, j])

    def others(body):
        def step(i, carry):
            body(lax.rem(me + i, PEERS))
            return carry
        lax.fori_loop(1, PEERS, step, 0)

    ready = set()
    first = True
    for g in (1, 2, 0, 3):
        for q in range(max(2 * g - 1, 0), min(2 * g + 3, 8)):
            if q not in ready:
                load(q).wait()
                ready.add(q)
        if g == 0:
            for h in halos:
                h.wait_recv()
            for q, (ref, inside) in ((0, (mlo, inside_lo)), (72, (mhi, inside_hi))):
                sea = ref[...].astype(jnp.float32) * inside
                for i in range(8):
                    seab[q + i] = jnp.broadcast_to(sea[i:i + 1, :], (8, COLS))
        propagate(g)
        if first:
            pl.semaphore_wait(barrier, PEERS + 1)
            for h in halos:
                h.start()
            first = False
        for j in (2 * g, 2 * g + 1):
            others(lambda d: forward(j, d).start())
            own(j).start()
        if g == 2:
            for w in weights:
                w.start()
            for i in range(NB // COLS):
                at = pl.ds(i * COLS, COLS)
                growb[at, :] = jnp.transpose(jnp.broadcast_to(0.25 * grow[i:i + 1, :] + 1.0, (COLS, COLS)))
                bandb[at, :] = jnp.transpose(jnp.broadcast_to(band[i:i + 1, :], (COLS, COLS)))
    for w in weights:
        w.wait()

    order = (2, 3, 4, 5, 0, 1, 6, 7)

    def sources(j):
        others(lambda d: arrival(j, d).wait_recv())
        own(j).wait()

        def prepare(i, total):
            at = pl.ds(pl.multiple_of(i * LB, LB), LB)
            field = got[j, at, :]
            state[at, :] = field.astype(jnp.bfloat16)
            square[at, :] = (field * field).astype(jnp.bfloat16)
            return total + jnp.sum((bandb[at, :] * field).reshape(LB // 8, 8, COLS), axis=0)
        energy = jnp.sum(lax.fori_loop(0, PEERS, prepare, jnp.zeros((8, COLS), jnp.float32)), axis=0, keepdims=True)
        damp = 1.0 / (1.0 + 0.5 * energy)

        def owner(i, carry):
            d = lax.rem(me + i, PEERS)
            at = pl.ds(pl.multiple_of(d * LB, LB), LB)
            gain = jnp.dot(kgv[at, :], state[...], preferred_element_type=jnp.float32)
            loss = jnp.dot(klv[at, :], square[...], preferred_element_type=jnp.float32)
            field = got[j, at, :]
            fresh[j, at, :] = (field * (growb[at, :] + 0.25 * gain) - 0.25 * loss) * damp

            @pl.when(i < PEERS)
            def _():
                give(j, d).start()
            return carry
        lax.fori_loop(1, PEERS + 1, owner, 0)
        keep(j).start()

    for j in order:
        sources(j)

    def save(j):
        return pltpu.make_async_copy(outv.at[:, pl.ds(8 * j, 8), :], out.at[:, pl.ds(8 * j, 8), :], out_sem.at[j])

    for j in order:
        others(lambda d: returned(j, d).wait_recv())
        keep(j).wait()
        sea = mask[8 * j:8 * j + 8, :].astype(jnp.float32)

        def turn(b, carry):
            outv[b, pl.ds(8 * j, 8), :] = back[pl.ds(8 * j * LB + b, 8, stride=LB), :] * sea
            return carry
        lax.fori_loop(0, LB, turn, 0, unroll=8)
        save(j).start()

    for h in halos:
        h.wait_send()
    for j in order:
        others(lambda d: forward(j, d).wait_send())
        others(lambda d: give(j, d).wait_send())
    for j in order:
        save(j).wait()


ORDER = (1, 2, 0, 3)
BASE = 13
EXT = 3
TILES = BASE * 4
CAP = BASE * COLS


def sea_kernel(x, mask, cosv, sinv, grow, band, kg, kl, out, flag,
               fin, seab, mlo, mhi, sent, extra, halves, place, hole_at, got, fresh, back, total, outv,
               kgv, klv, growb, bandb, state, square, flx, flz,
               load_sem, halo_send, halo_recv, fs, fr, bs, br, out_sem, fls, flr):
    me = lax.axis_index("bins")
    space = lax.axis_index("space")
    up = lax.rem(space + 1, SLABS)
    down = lax.rem(space + SLABS - 1, SLABS)
    core = lax.rem(me, 2)
    mine = slot_of(me)
    sx = lax.rem(space, 4)
    sz = space // 4
    f32, bf16 = jnp.float32, jnp.bfloat16

    def x_peer(i):
        return sz * 4 + lax.rem(sx + i, 4)

    def z_peer(i):
        return lax.rem(sz + i, 4) * 4 + sx

    barrier = pltpu.get_barrier_semaphore()
    for i in range(1, PEERS):
        pl.semaphore_signal(barrier, inc=1, device_id=(lax.rem(me + i, PEERS), space), device_id_type=MESH)
    for other in [up, down] + [x_peer(i) for i in (1, 2, 3)] + [z_peer(i) for i in (1, 2, 3)]:
        pl.semaphore_signal(barrier, inc=1, device_id=(me, other), device_id_type=MESH)

    def load(q):
        return pltpu.make_async_copy(x.at[:, pl.ds(8 * q, 8), :], fin.at[:, pl.ds(8 * q + 8, 8), :], load_sem.at[q])

    for q in (1, 2, 3, 4, 5, 6, 0, 7):
        load(q).start()
    weights = [pltpu.make_async_copy(kg, kgv, load_sem.at[8]), pltpu.make_async_copy(kl, klv, load_sem.at[9])]

    for q in range(ROWS // 8):
        sea = mask[8 * q:8 * q + 8, :].astype(f32)
        for i in range(8):
            seab[8 + 8 * q + i] = jnp.broadcast_to(sea[i:i + 1, :], (8, COLS))

    halos = [
        pltpu.make_async_remote_copy(x.at[:, pl.ds(56, 8), :], fin.at[:, pl.ds(0, 8), :], halo_send.at[0], halo_recv.at[0],
                                     device_id=(me, up), device_id_type=MESH),
        pltpu.make_async_remote_copy(x.at[:, pl.ds(0, 8), :], fin.at[:, pl.ds(72, 8), :], halo_send.at[1], halo_recv.at[1],
                                     device_id=(me, down), device_id_type=MESH),
        pltpu.make_async_remote_copy(mask.at[pl.ds(56, 8), :], mlo, halo_send.at[2], halo_recv.at[2],
                                     device_id=(me, up), device_id_type=MESH),
        pltpu.make_async_remote_copy(mask.at[pl.ds(0, 8), :], mhi, halo_send.at[3], halo_recv.at[3],
                                     device_id=(me, down), device_id_type=MESH),
    ]
    inside_lo = (space > 0).astype(f32)
    inside_hi = (space < SLABS - 1).astype(f32)
    flat = fin.reshape(LB * PAD, COLS)
    lane = lax.broadcasted_iota(jnp.int32, (8, COLS), 1)
    sub = lax.broadcasted_iota(jnp.int32, (8, COLS), 0)

    before = (lax.broadcasted_iota(jnp.int32, (COLS, COLS), 0) < lax.broadcasted_iota(jnp.int32, (COLS, COLS), 1)).astype(f32).astype(bf16)
    ones = jnp.ones((COLS, COLS), bf16)

    def assign(p):
        g = ORDER[p]
        sea = mask[16 * g:16 * g + 16, :].astype(f32)
        row = lax.broadcasted_iota(jnp.int32, (16, COLS), 0)
        pick = jnp.where(row < BASE, 1.0 - sea, sea)
        ranks = jnp.dot(pick.astype(bf16), before, preferred_element_type=f32)
        counts = jnp.dot(pick.astype(bf16), ones, preferred_element_type=f32)
        holes = jnp.zeros((1, COLS), f32)
        for i in range(BASE):
            hole_at[i:i + 1, :] = jnp.where(pick[i:i + 1] > 0.0, ranks[i:i + 1] + holes, -1.0)
            holes = holes + counts[i:i + 1]
        filled = jnp.zeros((1, COLS), f32)
        wants = []
        for i in range(BASE, 16):
            want = jnp.where(pick[i:i + 1] > 0.0, ranks[i:i + 1] + filled, -2.0)
            wants.append(jnp.transpose(jnp.broadcast_to(want, (COLS, COLS))))
            filled = filled + counts[i:i + 1]

        def one(i, carry):
            hole = hole_at[pl.ds(i, 1), :]
            for k in range(EXT):
                place[BASE * p + i, k * COLS:(k + 1) * COLS, :] = jnp.where(wants[k] == hole, 1.0, 0.0).astype(bf16)
            return carry
        lax.fori_loop(0, BASE, one, 0)
        return filled - holes

    def propagate(p):
        g = ORDER[p]

        def tile(t, carry):
            b0 = pl.multiple_of(t * 8, 8)
            rows = [flat[pl.ds(b0 * PAD + 16 * g + 4 + i, 8, stride=PAD), :] for i in range(24)]
            if g == 0:
                rows = [r * inside_lo for r in rows[:4]] + rows[4:]
            if g == 3:
                rows = rows[:20] + [r * inside_hi for r in rows[20:]]
            field = advance(jnp.stack(rows), b0, me, cosv, sinv, lane, sub, lambda step, n: seab[pl.ds(16 * g + 5 + step, n)])
            sent[pl.ds(BASE * p, BASE), pl.ds(b0, 8), :] = field[:BASE]
            extra[:, pl.ds(b0, 8), :] = field[BASE:]
            return carry
        lax.fori_loop(0, LB // 8, tile, 0, unroll=2)
        for k in range(EXT):
            cells = extra[k]
            high = cells.astype(bf16)
            halves[0:LB, k * COLS:(k + 1) * COLS] = high
            halves[LB:2 * LB, k * COLS:(k + 1) * COLS] = (cells - high.astype(f32)).astype(bf16)

    def forward(q):
        d = device_of(lax.rem(q, 8))
        return d, pltpu.make_async_remote_copy(
            sent.at[q], got.at[q // 8, pl.ds(me * LB, LB), :], fs.at[q], fr.at[q // 8, me],
            device_id=(d, space), device_id_type=MESH)

    def arrival(j, d):
        return pltpu.make_async_remote_copy(
            sent.at[0], got.at[j, pl.ds(d * LB, LB), :], fs.at[0], fr.at[j, d],
            device_id=(lax.rem(me + 1, PEERS), space), device_id_type=MESH)

    def seat(q):
        return ((q // BASE) * 16 + lax.rem(q, BASE)) * LB

    def give(j, d):
        return pltpu.make_async_remote_copy(
            fresh.at[j, pl.ds(d * LB, LB), :], back.at[pl.ds(seat(8 * j + mine), LB), :], bs.at[j, d], br.at[8 * j + mine],
            device_id=(d, space), device_id_type=MESH)

    def returned(q):
        return pltpu.make_async_remote_copy(
            fresh.at[0, pl.ds(0, LB), :], back.at[pl.ds(seat(q), LB), :], bs.at[0, 0], br.at[q],
            device_id=(lax.rem(me + 1, PEERS), space), device_id_type=MESH)

    def fill_and_send(p):
        def one(i, carry):
            q = BASE * p + i
            moved = jnp.dot(halves[...], place[q], preferred_element_type=f32)
            sent[q] = sent[q] + (moved[:LB] + moved[LB:])
            d, copy = forward(q)

            @pl.when(d != me)
            def _():
                copy.start()

            @pl.when(d == me)
            def _():
                pltpu.make_async_copy(sent.at[q], got.at[q // 8, pl.ds(me * LB, LB), :], fr.at[q // 8, me]).start()
            return carry
        lax.fori_loop(0, BASE, one, 0)

    ready = set()
    over = assign(0)
    for p, g in enumerate(ORDER):
        for q in range(max(2 * g - 1, 0), min(2 * g + 3, 8)):
            if q not in ready:
                load(q).wait()
                ready.add(q)
        if p == 2:
            for h in halos:
                h.wait_recv()
            for q, (ref, inside) in ((0, (mlo, inside_lo)), (72, (mhi, inside_hi))):
                sea = ref[...].astype(f32) * inside
                for i in range(8):
                    seab[q + i] = jnp.broadcast_to(sea[i:i + 1, :], (8, COLS))
        propagate(p)
        if p == 0:
            pl.semaphore_wait(barrier, PEERS + 7)
            for h in halos:
                h.start()
        fill_and_send(p)
        if p < 3:
            over = jnp.maximum(over, assign(p + 1))
        if p == 1:
            for w in weights:
                w.start()
            for i in range(NB // COLS):
                at = pl.ds(i * COLS, COLS)
                growb[at, :] = jnp.transpose(jnp.broadcast_to(0.25 * grow[i:i + 1, :] + 1.0, (COLS, COLS)))
                bandb[at, :] = jnp.transpose(jnp.broadcast_to(band[i:i + 1, :], (COLS, COLS)))

    def tell(stage, i):
        ref, at, to = ((flx, sx, x_peer(i)), (flz, sz, z_peer(i)))[stage]
        return pltpu.make_async_remote_copy(ref.at[at], ref.at[at], fls.at[stage, i], flr.at[stage, at],
                                            device_id=(me, to), device_id_type=MESH)

    def told(stage, i):
        ref, at, to = ((flx, sx, x_peer(i)), (flz, sz, z_peer(i)))[stage]
        at = lax.rem(at + i, 4)
        return pltpu.make_async_remote_copy(ref.at[at], ref.at[at], fls.at[stage, i], flr.at[stage, at],
                                            device_id=(me, to), device_id_type=MESH)

    flx[sx] = jnp.broadcast_to(over, (8, COLS))
    for i in (1, 2, 3):
        tell(0, i).start()
    for w in weights:
        w.wait()

    def sources(j):
        def each(d, carry):
            arrival(j, d).wait_recv()
            return carry
        lax.fori_loop(0, PEERS, each, 0)

        def prepare(i, total):
            at = pl.ds(pl.multiple_of(i * LB, LB), LB)
            field = got[j, at, :]
            state[at, :] = field.astype(bf16)
            square[at, :] = (field * field).astype(bf16)
            return total + jnp.sum((bandb[at, :] * field).reshape(LB // 8, 8, COLS), axis=0)
        energy = jnp.sum(lax.fori_loop(0, PEERS, prepare, jnp.zeros((8, COLS), f32)), axis=0, keepdims=True)
        damp = 1.0 / (1.0 + 0.5 * energy)

        def owner(i, carry):
            d = lax.rem(me + i, PEERS)
            at = pl.ds(pl.multiple_of(d * LB, LB), LB)
            gain = jnp.dot(kgv[at, :], state[...], preferred_element_type=f32)
            loss = jnp.dot(klv[at, :], square[...], preferred_element_type=f32)
            field = got[j, at, :]
            fresh[j, at, :] = (field * (growb[at, :] + 0.25 * gain) - 0.25 * loss) * damp

            @pl.when(i < PEERS)
            def _():
                give(j, d).start()
            return carry
        lax.fori_loop(1, PEERS + 1, owner, 0)
        pltpu.make_async_copy(
            fresh.at[j, pl.ds(me * LB, LB), :], back.at[pl.ds(seat(8 * j + mine), LB), :], br.at[8 * j + mine]).start()

    def full_rounds(j, carry):
        sources(j)
        return carry
    lax.fori_loop(0, 6, full_rounds, 0)

    @pl.when(core == 0)
    def _():
        sources(6)

    for i in (1, 2, 3):
        told(0, i).wait_recv()
    flz[sz] = jnp.maximum(jnp.maximum(flx[0], flx[1]), jnp.maximum(flx[2], flx[3]))
    for i in (1, 2, 3):
        tell(1, i).start()

    def save(q):
        return pltpu.make_async_copy(outv.at[:, pl.ds(8 * q, 8), :], out.at[:, pl.ds(8 * q, 8), :], out_sem.at[q])

    for p, g in enumerate(ORDER):
        total[...] = jnp.zeros_like(total)

        def pull(i, carry):
            q = BASE * p + i
            returned(q).wait_recv()
            cells = back[pl.ds(pl.multiple_of((16 * p + i) * LB, LB), LB), :]
            high = cells.astype(bf16)
            low = (cells - high.astype(f32)).astype(bf16)
            both = jnp.concatenate([high, low], axis=0)
            total[...] += lax.dot_general(both, place[q], (((1,), (1,)), ((), ())), preferred_element_type=f32)
            return carry
        lax.fori_loop(0, BASE, pull, 0)
        for k in range(EXT):
            at = slice(k * COLS, (k + 1) * COLS)
            back[pl.ds((16 * p + BASE + k) * LB, LB), :] = total[:LB, at] + total[LB:, at]
        for h in (0, 1):
            r0 = 16 * g + 8 * h
            sea = mask[r0:r0 + 8, :].astype(f32)

            def turn(b, carry):
                outv[b, pl.ds(r0, 8), :] = back[pl.ds((16 * p + 8 * h) * LB + b, 8, stride=LB), :] * sea
                return carry
            lax.fori_loop(0, LB, turn, 0, unroll=8)
            save(2 * g + h).start()

    for i in (1, 2, 3):
        told(1, i).wait_recv()
    flag[...] = jnp.maximum(jnp.maximum(flz[0], flz[1]), jnp.maximum(flz[2], flz[3]))
    for h in halos:
        h.wait_send()
    for i in (1, 2, 3):
        tell(0, i).wait_send()
        tell(1, i).wait_send()

    def drain(q, carry):
        d, copy = forward(q)

        @pl.when(d != me)
        def _():
            copy.wait_send()
        return carry
    lax.fori_loop(0, TILES, drain, 0)

    def drain_round(j):
        def step(i, carry):
            give(j, lax.rem(me + i, PEERS)).wait_send()
            return carry
        lax.fori_loop(1, PEERS, step, 0)

    for j in range(6):
        drain_round(j)

    @pl.when(core == 0)
    def _():
        drain_round(6)
    for q in range(8):
        save(q).wait()


def finish_kernel(packed, out, staged, load_sem, save_sem):
    part = LB // 12
    loads, saves = [], []
    for i in range(12):
        at = pl.ds(i * part, part)
        loads.append(pltpu.make_async_copy(packed.at[at], staged.at[at], load_sem.at[i]))
        saves.append(pltpu.make_async_copy(staged.at[at], out.at[at], save_sem.at[i]))
    for load in loads:
        load.start()
    for load, save in zip(loads, saves):
        load.wait()
        save.start()
    for save in saves:
        save.wait()


def local(spectra, land_mask, growth, band_weight, kernel_gain, kernel_loss):
    theta = 2.0 * math.pi * (np.arange(LB) % ND + 0.5) / ND
    wide = lambda v: jnp.asarray(np.repeat(v.astype(np.float32)[:, None], COLS, 1))
    vmem = pl.BlockSpec(memory_space=pltpu.VMEM)
    anym = pl.BlockSpec(memory_space=pl.ANY)
    f32, bf16, i32 = jnp.float32, jnp.bfloat16, jnp.int32
    dma = pltpu.SemaphoreType.DMA
    shape = jax.ShapeDtypeStruct((LB, ROWS, COLS), f32)
    operands = (spectra, land_mask, wide(np.cos(theta)), wide(np.sin(theta)),
                growth.reshape(NB // COLS, COLS), band_weight.reshape(NB // COLS, COLS), kernel_gain, kernel_loss)
    in_specs = [anym, vmem, vmem, vmem, vmem, vmem, anym, anym]
    weights = [
        pltpu.VMEM((NB, NB), bf16),
        pltpu.VMEM((NB, NB), bf16),
        pltpu.VMEM((NB, COLS), f32),
        pltpu.VMEM((NB, COLS), f32),
        pltpu.VMEM((NB, COLS), bf16),
        pltpu.VMEM((NB, COLS), bf16),
    ]
    edges = [
        pltpu.VMEM((LB, PAD, COLS), f32),
        pltpu.VMEM((PAD, 8, COLS), f32),
        pltpu.VMEM((8, COLS), i32),
        pltpu.VMEM((8, COLS), i32),
    ]

    def finish(packed):
        return pl.pallas_call(
            finish_kernel,
            out_shape=shape,
            in_specs=[anym],
            out_specs=anym,
            scratch_shapes=[pltpu.VMEM((LB, ROWS, COLS), f32), dma((12,)), dma((12,))],
            compiler_params=pltpu.CompilerParams(vmem_limit_bytes=62 * 2**20),
        )(packed)

    def whole(args):
        return finish(pl.pallas_call(
            whole_kernel,
            out_shape=shape,
            in_specs=in_specs,
            out_specs=anym,
            scratch_shapes=edges + [
                pltpu.VMEM((ROWS, LB, COLS), f32),
                pltpu.VMEM((ROUNDS, NB, COLS), f32),
                pltpu.VMEM((ROUNDS, NB, COLS), f32),
                pltpu.VMEM((ROWS * LB, COLS), f32),
                pltpu.VMEM((LB, ROWS, COLS), f32),
            ] + weights + [
                dma((10,)), dma((4,)), dma((4,)), dma((2, ROUNDS)),
                dma((ROUNDS, PEERS)), dma((ROUNDS, PEERS)), dma((ROUNDS, PEERS)), dma((ROUNDS, PEERS)),
                dma((ROUNDS,)),
            ],
            compiler_params=pltpu.CompilerParams(collective_id=1, has_side_effects=True, vmem_limit_bytes=62 * 2**20),
        )(*args[1:]))

    packed, flag = pl.pallas_call(
        sea_kernel,
        out_shape=(shape, pltpu.VMEM((8, COLS), f32)),
        in_specs=in_specs,
        out_specs=(anym, vmem),
        scratch_shapes=edges + [
            pltpu.VMEM((TILES, LB, COLS), f32),
            pltpu.VMEM((EXT, LB, COLS), f32),
            pltpu.VMEM((2 * LB, EXT * COLS), bf16),
            pltpu.VMEM((TILES, EXT * COLS, COLS), bf16),
            pltpu.VMEM((16, COLS), f32),
            pltpu.VMEM((7, NB, COLS), f32),
            pltpu.VMEM((7, NB, COLS), f32),
            pltpu.VMEM((ROWS * LB, COLS), f32),
            pltpu.VMEM((2 * LB, EXT * COLS), f32),
            pltpu.VMEM((LB, ROWS, COLS), f32),
        ] + weights + [
            pltpu.VMEM((4, 8, COLS), f32),
            pltpu.VMEM((4, 8, COLS), f32),
            dma((10,)), dma((4,)), dma((4,)),
            dma((TILES,)), dma((7, PEERS)), dma((7, PEERS)), dma((TILES,)),
            dma((8,)), dma((2, 4)), dma((2, 4)),
        ],
        compiler_params=pltpu.CompilerParams(collective_id=0, has_side_effects=True, vmem_limit_bytes=62 * 2**20),
    )(*operands)
    return lax.cond(flag[0, 0] > 0.0, whole, lambda args: finish(args[0]), (packed,) + operands)


def solution(mesh):
    in_specs = (P("bins", "space", None), P("space", None), P(), P(), P(), P())
    out_specs = P("bins", "space", None)
    return jax.shard_map(local, mesh=mesh, in_specs=in_specs, out_specs=out_specs, check_vma=False)
```

```python
import functools
import math

import jax
import jax.numpy as jnp
import numpy as np
from jax import lax
from jax.experimental import pallas as pl
from jax.experimental.pallas import tpu as pltpu
from jax.sharding import PartitionSpec as P

NF = 32
ND = 36
SUBSTEPS = 4
PEERS = 8
SLABS = 16
LB = 144
NB = 1152
ROWS = 64
COLS = 128
PAD = ROWS + 16
ROUNDS = 8
MESH = pl.DeviceIdType.MESH


def device_of(slot):
    return (slot % 4) * 2 + slot // 4


def slot_of(device):
    return device // 2 + 4 * lax.rem(device, 2)


def advance(field, b0, me, cosv, sinv, lane, sub, sea):
    b = sub + b0
    one = lambda c: c.astype(jnp.float32)
    freq = (4 * me).astype(jnp.float32) + one(b >= ND) + one(b >= 2 * ND) + one(b >= 3 * ND)
    group = 0.9 / (1.0 + 2.3 * freq / max(NF - 1, 1))
    cx = group * cosv[pl.ds(b0, 8), :]
    cy = group * sinv[pl.ds(b0, 8), :]
    right, ahead = cx > 0.0, cy > 0.0
    ax, ay = jnp.abs(cx), jnp.abs(cy)
    stay = 1.0 - ay
    move = jnp.where((ahead & (lane == 0)) | (~ahead & (lane == COLS - 1)), 0.0, ay)
    for step in range(SUBSTEPS):
        n = field.shape[0] - 2
        mid = field[1:-1]
        near = jnp.where(right[None], field[:-2], field[2:])
        mid = mid + ax[None] * (near - mid)
        near = jnp.stack([jnp.where(ahead, pltpu.roll(mid[i], 1, 1), pltpu.roll(mid[i], COLS - 1, 1)) for i in range(n)])
        field = (stay[None] * mid + move[None] * near) * sea(step, n)
    return field


def whole_kernel(x, mask, cosv, sinv, grow, band, kg, kl, out,
           fin, seab, mlo, mhi, sent, got, fresh, back, kgv, klv, growb, bandb, state, square,
           load_sem, halo_send, halo_recv, own_sem, fs, fr, bs, br):
    me = lax.axis_index("bins")
    space = lax.axis_index("space")
    up = lax.rem(space + 1, SLABS)
    down = lax.rem(space + SLABS - 1, SLABS)

    barrier = pltpu.get_barrier_semaphore()
    for i in range(1, PEERS):
        pl.semaphore_signal(barrier, inc=1, device_id=(lax.rem(me + i, PEERS), space), device_id_type=MESH)
    for other in (up, down):
        pl.semaphore_signal(barrier, inc=1, device_id=(me, other), device_id_type=MESH)

    def load(q):
        return pltpu.make_async_copy(x.at[:, pl.ds(8 * q, 8), :], fin.at[:, pl.ds(8 * q + 8, 8), :], load_sem.at[q])

    for q in (1, 2, 3, 4, 5, 6, 0, 7):
        load(q).start()
    weights = [pltpu.make_async_copy(kg, kgv, load_sem.at[8]), pltpu.make_async_copy(kl, klv, load_sem.at[9])]

    for q in range(ROWS // 8):
        sea = mask[8 * q:8 * q + 8, :].astype(jnp.float32)
        for i in range(8):
            seab[8 + 8 * q + i] = jnp.broadcast_to(sea[i:i + 1, :], (8, COLS))

    halos = [
        pltpu.make_async_remote_copy(x.at[:, pl.ds(56, 8), :], fin.at[:, pl.ds(0, 8), :], halo_send.at[0], halo_recv.at[0],
                                     device_id=(me, up), device_id_type=MESH),
        pltpu.make_async_remote_copy(x.at[:, pl.ds(0, 8), :], fin.at[:, pl.ds(72, 8), :], halo_send.at[1], halo_recv.at[1],
                                     device_id=(me, down), device_id_type=MESH),
        pltpu.make_async_remote_copy(mask.at[pl.ds(56, 8), :], mlo, halo_send.at[2], halo_recv.at[2],
                                     device_id=(me, up), device_id_type=MESH),
        pltpu.make_async_remote_copy(mask.at[pl.ds(0, 8), :], mhi, halo_send.at[3], halo_recv.at[3],
                                     device_id=(me, down), device_id_type=MESH),
    ]
    inside_lo = (space > 0).astype(jnp.float32)
    inside_hi = (space < SLABS - 1).astype(jnp.float32)
    flat = fin.reshape(LB * PAD, COLS)
    lane = lax.broadcasted_iota(jnp.int32, (8, COLS), 1)
    sub = lax.broadcasted_iota(jnp.int32, (8, COLS), 0)

    def propagate(g):
        def tile(t, carry):
            b0 = pl.multiple_of(t * 8, 8)
            rows = [flat[pl.ds(b0 * PAD + 16 * g + 4 + i, 8, stride=PAD), :] for i in range(24)]
            if g == 0:
                rows = [r * inside_lo for r in rows[:4]] + rows[4:]
            if g == 3:
                rows = rows[:20] + [r * inside_hi for r in rows[20:]]
            field = jnp.stack(rows)
            field = advance(field, b0, me, cosv, sinv, lane, sub, lambda step, n: seab[pl.ds(16 * g + 5 + step, n)])
            sent[pl.ds(16 * g, 16), pl.ds(b0, 8), :] = field
            return carry
        lax.fori_loop(0, LB // 8, tile, 0, unroll=2)

    def forward(j, d):
        row = 8 * j + slot_of(d)
        return pltpu.make_async_remote_copy(
            sent.at[row], got.at[j, pl.ds(me * LB, LB), :], fs.at[j, d], fr.at[j, me],
            device_id=(d, space), device_id_type=MESH)

    def arrival(j, d):
        return pltpu.make_async_remote_copy(
            sent.at[0], got.at[j, pl.ds(d * LB, LB), :], fs.at[j, d], fr.at[j, d],
            device_id=(d, space), device_id_type=MESH)

    def own(j):
        return pltpu.make_async_copy(sent.at[8 * j + slot_of(me)], got.at[j, pl.ds(me * LB, LB), :], own_sem.at[0, j])

    def give(j, d):
        return pltpu.make_async_remote_copy(
            fresh.at[j, pl.ds(d * LB, LB), :], back.at[pl.ds((8 * j + slot_of(me)) * LB, LB), :], bs.at[j, d], br.at[j, me],
            device_id=(d, space), device_id_type=MESH)

    def returned(j, d):
        return pltpu.make_async_remote_copy(
            fresh.at[j, pl.ds(d * LB, LB), :], back.at[pl.ds((8 * j + slot_of(d)) * LB, LB), :], bs.at[j, d], br.at[j, d],
            device_id=(d, space), device_id_type=MESH)

    def keep(j):
        return pltpu.make_async_copy(
            fresh.at[j, pl.ds(me * LB, LB), :], back.at[pl.ds((8 * j + slot_of(me)) * LB, LB), :], own_sem.at[1, j])

    def others(body):
        def step(i, carry):
            body(lax.rem(me + i, PEERS))
            return carry
        lax.fori_loop(1, PEERS, step, 0)

    ready = set()
    first = True
    for g in (1, 2, 0, 3):
        for q in range(max(2 * g - 1, 0), min(2 * g + 3, 8)):
            if q not in ready:
                load(q).wait()
                ready.add(q)
        if g == 0:
            for h in halos:
                h.wait_recv()
            for q, (ref, inside) in ((0, (mlo, inside_lo)), (72, (mhi, inside_hi))):
                sea = ref[...].astype(jnp.float32) * inside
                for i in range(8):
                    seab[q + i] = jnp.broadcast_to(sea[i:i + 1, :], (8, COLS))
        propagate(g)
        if first:
            pl.semaphore_wait(barrier, PEERS + 1)
            for h in halos:
                h.start()
            first = False
        for j in (2 * g, 2 * g + 1):
            others(lambda d: forward(j, d).start())
            own(j).start()
        if g == 2:
            for w in weights:
                w.start()
            for i in range(NB // COLS):
                at = pl.ds(i * COLS, COLS)
                growb[at, :] = jnp.transpose(jnp.broadcast_to(0.25 * grow[i:i + 1, :] + 1.0, (COLS, COLS)))
                bandb[at, :] = jnp.transpose(jnp.broadcast_to(band[i:i + 1, :], (COLS, COLS)))
    for w in weights:
        w.wait()

    order = (2, 3, 4, 5, 0, 1, 6, 7)

    def sources(j):
        others(lambda d: arrival(j, d).wait_recv())
        own(j).wait()

        def prepare(i, total):
            at = pl.ds(pl.multiple_of(i * LB, LB), LB)
            field = got[j, at, :]
            state[at, :] = field.astype(jnp.bfloat16)
            square[at, :] = (field * field).astype(jnp.bfloat16)
            return total + jnp.sum((bandb[at, :] * field).reshape(LB // 8, 8, COLS), axis=0)
        energy = jnp.sum(lax.fori_loop(0, PEERS, prepare, jnp.zeros((8, COLS), jnp.float32)), axis=0, keepdims=True)
        damp = 1.0 / (1.0 + 0.5 * energy)

        def owner(i, carry):
            d = lax.rem(me + i, PEERS)
            at = pl.ds(pl.multiple_of(d * LB, LB), LB)
            gain = jnp.dot(kgv[at, :], state[...], preferred_element_type=jnp.float32)
            loss = jnp.dot(klv[at, :], square[...], preferred_element_type=jnp.float32)
            field = got[j, at, :]
            fresh[j, at, :] = (field * (growb[at, :] + 0.25 * gain) - 0.25 * loss) * damp

            @pl.when(i < PEERS)
            def _():
                give(j, d).start()
            return carry
        lax.fori_loop(1, PEERS + 1, owner, 0)
        keep(j).start()

    for j in order:
        sources(j)

    for j in order:
        others(lambda d: returned(j, d).wait_recv())
        keep(j).wait()
        sea = mask[8 * j:8 * j + 8, :].astype(jnp.float32)

        def turn(b, carry):
            out[b, pl.ds(8 * j, 8), :] = back[pl.ds(8 * j * LB + b, 8, stride=LB), :] * sea
            return carry
        lax.fori_loop(0, LB, turn, 0, unroll=8)

    for h in halos:
        h.wait_send()
    for j in order:
        others(lambda d: forward(j, d).wait_send())
        others(lambda d: give(j, d).wait_send())


ORDER = (1, 2, 0, 3)
BASE = 13
EXT = 3
TILES = BASE * 4
SPLIT = 80


def sea_kernel(x, mask, cosv, sinv, grow, band, kg, kl, out, flag,
               fin, seab, mlo, mhi, sent, extra, halves, place, hole_at, got, fresh, back, total,
               kgv, klv, growb, bandb, state, square, flx, flz,
               load_sem, halo_send, halo_recv, fs, fr, bs, br, fls, flr):
    me = lax.axis_index("bins")
    space = lax.axis_index("space")
    up = lax.rem(space + 1, SLABS)
    down = lax.rem(space + SLABS - 1, SLABS)
    core = lax.rem(me, 2)
    mine = slot_of(me)
    sx = lax.rem(space, 4)
    sz = space // 4
    f32, bf16 = jnp.float32, jnp.bfloat16

    def x_peer(i):
        return sz * 4 + lax.rem(sx + i, 4)

    def z_peer(i):
        return lax.rem(sz + i, 4) * 4 + sx

    barrier = pltpu.get_barrier_semaphore()
    for i in range(1, PEERS):
        pl.semaphore_signal(barrier, inc=1, device_id=(lax.rem(me + i, PEERS), space), device_id_type=MESH)
    for other in [up, down] + [x_peer(i) for i in (1, 2, 3)] + [z_peer(i) for i in (1, 2, 3)]:
        pl.semaphore_signal(barrier, inc=1, device_id=(me, other), device_id_type=MESH)

    def load(q):
        return pltpu.make_async_copy(x.at[:, pl.ds(8 * q, 8), :], fin.at[:, pl.ds(8 * q + 8, 8), :], load_sem.at[q])

    for q in (1, 2, 3, 4, 5, 6, 0, 7):
        load(q).start()
    weights = [pltpu.make_async_copy(kg, kgv, load_sem.at[8]), pltpu.make_async_copy(kl, klv, load_sem.at[9])]

    for q in range(ROWS // 8):
        sea = mask[8 * q:8 * q + 8, :].astype(f32)
        for i in range(8):
            seab[8 + 8 * q + i] = jnp.broadcast_to(sea[i:i + 1, :], (8, COLS))

    halos = [
        pltpu.make_async_remote_copy(x.at[:, pl.ds(56, 8), :], fin.at[:, pl.ds(0, 8), :], halo_send.at[0], halo_recv.at[0],
                                     device_id=(me, up), device_id_type=MESH),
        pltpu.make_async_remote_copy(x.at[:, pl.ds(0, 8), :], fin.at[:, pl.ds(72, 8), :], halo_send.at[1], halo_recv.at[1],
                                     device_id=(me, down), device_id_type=MESH),
        pltpu.make_async_remote_copy(mask.at[pl.ds(56, 8), :], mlo, halo_send.at[2], halo_recv.at[2],
                                     device_id=(me, up), device_id_type=MESH),
        pltpu.make_async_remote_copy(mask.at[pl.ds(0, 8), :], mhi, halo_send.at[3], halo_recv.at[3],
                                     device_id=(me, down), device_id_type=MESH),
    ]
    inside_lo = (space > 0).astype(f32)
    inside_hi = (space < SLABS - 1).astype(f32)
    flat = fin.reshape(LB * PAD, COLS)
    lane = lax.broadcasted_iota(jnp.int32, (8, COLS), 1)
    sub = lax.broadcasted_iota(jnp.int32, (8, COLS), 0)

    before = (lax.broadcasted_iota(jnp.int32, (COLS, COLS), 0) < lax.broadcasted_iota(jnp.int32, (COLS, COLS), 1)).astype(f32).astype(bf16)
    ones = jnp.ones((COLS, COLS), bf16)

    def assign(p):
        g = ORDER[p]
        sea = mask[16 * g:16 * g + 16, :].astype(f32)
        row = lax.broadcasted_iota(jnp.int32, (16, COLS), 0)
        pick = jnp.where(row < BASE, 1.0 - sea, sea)
        ranks = jnp.dot(pick.astype(bf16), before, preferred_element_type=f32)
        counts = jnp.dot(pick.astype(bf16), ones, preferred_element_type=f32)
        holes = jnp.zeros((1, COLS), f32)
        for i in range(BASE):
            hole_at[i:i + 1, :] = jnp.where(pick[i:i + 1] > 0.0, ranks[i:i + 1] + holes, -1.0)
            holes = holes + counts[i:i + 1]
        filled = jnp.zeros((1, COLS), f32)
        wants = []
        for i in range(BASE, 16):
            want = jnp.where(pick[i:i + 1] > 0.0, ranks[i:i + 1] + filled, -2.0)
            wants.append(jnp.transpose(jnp.broadcast_to(want, (COLS, COLS))))
            filled = filled + counts[i:i + 1]

        def one(i, carry):
            hole = hole_at[pl.ds(i, 1), :]
            for k in range(EXT):
                place[BASE * p + i, k * COLS:(k + 1) * COLS, :] = jnp.where(wants[k] == hole, 1.0, 0.0).astype(bf16)
            return carry
        lax.fori_loop(0, BASE, one, 0)
        return filled - holes

    def propagate(p, lo, hi):
        g = ORDER[p]

        def tile(t, carry):
            b0 = pl.multiple_of(lo + t * 8, 8)
            rows = [flat[pl.ds(b0 * PAD + 16 * g + 4 + i, 8, stride=PAD), :] for i in range(24)]
            if g == 0:
                rows = [r * inside_lo for r in rows[:4]] + rows[4:]
            if g == 3:
                rows = rows[:20] + [r * inside_hi for r in rows[20:]]
            field = advance(jnp.stack(rows), b0, me, cosv, sinv, lane, sub, lambda step, n: seab[pl.ds(16 * g + 5 + step, n)])
            sent[pl.ds(BASE * p, BASE), pl.ds(b0, 8), :] = field[:BASE]
            extra[:, pl.ds(b0, 8), :] = field[BASE:]
            return carry
        lax.fori_loop(0, (hi - lo) // 8, tile, 0, unroll=2)
        for k in range(EXT):
            cells = extra[k, lo:hi, :]
            high = cells.astype(bf16)
            halves[2 * lo:lo + hi, k * COLS:(k + 1) * COLS] = high
            halves[lo + hi:2 * hi, k * COLS:(k + 1) * COLS] = (cells - high.astype(f32)).astype(bf16)

    def forward(q, lo=0, hi=LB):
        d = device_of(lax.rem(q, 8))
        return d, pltpu.make_async_remote_copy(
            sent.at[q, pl.ds(lo, hi - lo), :], got.at[q // 8, pl.ds(me * LB + lo, hi - lo), :], fs.at[q], fr.at[q // 8, me],
            device_id=(d, space), device_id_type=MESH)

    def arrival(j, d):
        return pltpu.make_async_remote_copy(
            sent.at[0], got.at[j, pl.ds(d * LB, LB), :], fs.at[0], fr.at[j, d],
            device_id=(lax.rem(me + 1, PEERS), space), device_id_type=MESH)

    def seat(q):
        return ((q // BASE) * 16 + lax.rem(q, BASE)) * LB

    def give(j, d):
        return pltpu.make_async_remote_copy(
            fresh.at[j, pl.ds(d * LB, LB), :], back.at[pl.ds(seat(8 * j + mine), LB), :], bs.at[j, d], br.at[8 * j + mine],
            device_id=(d, space), device_id_type=MESH)

    def returned(q):
        return pltpu.make_async_remote_copy(
            fresh.at[0, pl.ds(0, LB), :], back.at[pl.ds(seat(q), LB), :], bs.at[0, 0], br.at[q],
            device_id=(lax.rem(me + 1, PEERS), space), device_id_type=MESH)

    def fill_and_send(p, lo, hi):
        n = hi - lo
        at = pl.ds(lo, n)

        def one(i, carry):
            q = BASE * p + i
            moved = jnp.dot(halves[2 * lo:2 * hi, :], place[q], preferred_element_type=f32)
            sent[q, at, :] = sent[q, at, :] + (moved[:n] + moved[n:])
            d, copy = forward(q, lo, hi)

            @pl.when(d != me)
            def _():
                copy.start()

            @pl.when(d == me)
            def _():
                pltpu.make_async_copy(sent.at[q, at, :], got.at[q // 8, pl.ds(me * LB + lo, n), :], fr.at[q // 8, me]).start()
            return carry
        lax.fori_loop(0, BASE, one, 0)

    ready = set()
    over = assign(0)
    for p, g in enumerate(ORDER):
        for q in range(max(2 * g - 1, 0), min(2 * g + 3, 8)):
            if q not in ready:
                load(q).wait()
                ready.add(q)
        if p == 2:
            for h in halos:
                h.wait_recv()
            for q, (ref, inside) in ((0, (mlo, inside_lo)), (72, (mhi, inside_hi))):
                sea = ref[...].astype(f32) * inside
                for i in range(8):
                    seab[q + i] = jnp.broadcast_to(sea[i:i + 1, :], (8, COLS))
        for lo, hi in ((0, SPLIT), (SPLIT, LB)) if p == 0 else ((0, LB),):
            propagate(p, lo, hi)
            if p == 0 and lo == 0:
                pl.semaphore_wait(barrier, PEERS + 7)
                for h in halos:
                    h.start()
            fill_and_send(p, lo, hi)
        if p < 3:
            over = jnp.maximum(over, assign(p + 1))
        if p == 1:
            for w in weights:
                w.start()
            for i in range(NB // COLS):
                at = pl.ds(i * COLS, COLS)
                growb[at, :] = jnp.transpose(jnp.broadcast_to(0.25 * grow[i:i + 1, :] + 1.0, (COLS, COLS)))
                bandb[at, :] = jnp.transpose(jnp.broadcast_to(band[i:i + 1, :], (COLS, COLS)))

    def tell(stage, i):
        ref, at, to = ((flx, sx, x_peer(i)), (flz, sz, z_peer(i)))[stage]
        return pltpu.make_async_remote_copy(ref.at[at], ref.at[at], fls.at[stage, i], flr.at[stage, at],
                                            device_id=(me, to), device_id_type=MESH)

    def told(stage, i):
        ref, at, to = ((flx, sx, x_peer(i)), (flz, sz, z_peer(i)))[stage]
        at = lax.rem(at + i, 4)
        return pltpu.make_async_remote_copy(ref.at[at], ref.at[at], fls.at[stage, i], flr.at[stage, at],
                                            device_id=(me, to), device_id_type=MESH)

    flx[sx] = jnp.broadcast_to(over, (8, COLS))
    for i in (1, 2, 3):
        tell(0, i).start()
    for w in weights:
        w.wait()

    def sources(j):
        def each(d, carry):
            arrival(j, d).wait_recv()
            return carry
        lax.fori_loop(0, PEERS, each, 0)

        def prepare(i, total):
            at = pl.ds(pl.multiple_of(i * LB, LB), LB)
            field = got[j, at, :]
            state[at, :] = field.astype(bf16)
            square[at, :] = (field * field).astype(bf16)
            return total + jnp.sum((bandb[at, :] * field).reshape(LB // 8, 8, COLS), axis=0)
        energy = jnp.sum(lax.fori_loop(0, PEERS, prepare, jnp.zeros((8, COLS), f32)), axis=0, keepdims=True)
        damp = 1.0 / (1.0 + 0.5 * energy)

        def owner(i, carry):
            d = lax.rem(me + i, PEERS)
            at = pl.ds(pl.multiple_of(d * LB, LB), LB)
            gain = jnp.dot(kgv[at, :], state[...], preferred_element_type=f32)
            loss = jnp.dot(klv[at, :], square[...], preferred_element_type=f32)
            field = got[j, at, :]
            fresh[j, at, :] = (field * (growb[at, :] + 0.25 * gain) - 0.25 * loss) * damp

            @pl.when(i < PEERS)
            def _():
                give(j, d).start()
            return carry
        lax.fori_loop(1, PEERS + 1, owner, 0)
        pltpu.make_async_copy(
            fresh.at[j, pl.ds(me * LB, LB), :], back.at[pl.ds(seat(8 * j + mine), LB), :], br.at[8 * j + mine]).start()

    def full_rounds(j, carry):
        sources(j)
        return carry
    lax.fori_loop(0, 6, full_rounds, 0)

    @pl.when(core == 0)
    def _():
        sources(6)

    for i in (1, 2, 3):
        told(0, i).wait_recv()
    flz[sz] = jnp.maximum(jnp.maximum(flx[0], flx[1]), jnp.maximum(flx[2], flx[3]))
    for i in (1, 2, 3):
        tell(1, i).start()

    for p, g in enumerate(ORDER):
        total[...] = jnp.zeros_like(total)

        def pull(i, carry):
            q = BASE * p + i
            returned(q).wait_recv()
            cells = back[pl.ds(pl.multiple_of((16 * p + i) * LB, LB), LB), :]
            high = cells.astype(bf16)
            low = (cells - high.astype(f32)).astype(bf16)
            both = jnp.concatenate([high, low], axis=0)
            total[...] += lax.dot_general(both, place[q], (((1,), (1,)), ((), ())), preferred_element_type=f32)
            return carry
        lax.fori_loop(0, BASE, pull, 0)
        for k in range(EXT):
            at = slice(k * COLS, (k + 1) * COLS)
            back[pl.ds((16 * p + BASE + k) * LB, LB), :] = total[:LB, at] + total[LB:, at]
        for h in (0, 1):
            r0 = 16 * g + 8 * h
            sea = mask[r0:r0 + 8, :].astype(f32)

            def turn(b, carry):
                out[b, pl.ds(r0, 8), :] = back[pl.ds((16 * p + 8 * h) * LB + b, 8, stride=LB), :] * sea
                return carry
            lax.fori_loop(0, LB, turn, 0, unroll=8)

    for i in (1, 2, 3):
        told(1, i).wait_recv()
    flag[...] = jnp.maximum(jnp.maximum(flz[0], flz[1]), jnp.maximum(flz[2], flz[3]))
    for h in halos:
        h.wait_send()
    for i in (1, 2, 3):
        tell(0, i).wait_send()
        tell(1, i).wait_send()

    def drain(q, carry):
        d, copy = forward(q)

        @pl.when(d != me)
        def _():
            copy.wait_send()
        return carry
    lax.fori_loop(0, TILES, drain, 0)

    def drain_round(j):
        def step(i, carry):
            give(j, lax.rem(me + i, PEERS)).wait_send()
            return carry
        lax.fori_loop(1, PEERS, step, 0)

    for j in range(6):
        drain_round(j)

    @pl.when(core == 0)
    def _():
        drain_round(6)


def finish_kernel(packed, out, sems):
    part = LB // 8
    copies = [pltpu.make_async_copy(packed.at[pl.ds(i * part, part)], out.at[pl.ds(i * part, part)], sems.at[i]) for i in range(8)]
    for copy in copies:
        copy.start()
    for copy in copies:
        copy.wait()


def local(spectra, land_mask, growth, band_weight, kernel_gain, kernel_loss):
    theta = 2.0 * math.pi * (np.arange(LB) % ND + 0.5) / ND
    wide = lambda v: jnp.asarray(np.repeat(v.astype(np.float32)[:, None], COLS, 1))
    vmem = pl.BlockSpec(memory_space=pltpu.VMEM)
    anym = pl.BlockSpec(memory_space=pl.ANY)
    f32, bf16, i32 = jnp.float32, jnp.bfloat16, jnp.int32
    dma = pltpu.SemaphoreType.DMA
    shape = jax.ShapeDtypeStruct((LB, ROWS, COLS), f32)
    operands = (spectra, land_mask, wide(np.cos(theta)), wide(np.sin(theta)),
                growth.reshape(NB // COLS, COLS), band_weight.reshape(NB // COLS, COLS), kernel_gain, kernel_loss)
    in_specs = [anym, vmem, vmem, vmem, vmem, vmem, anym, anym]
    weights = [
        pltpu.VMEM((NB, NB), bf16),
        pltpu.VMEM((NB, NB), bf16),
        pltpu.VMEM((NB, COLS), f32),
        pltpu.VMEM((NB, COLS), f32),
        pltpu.VMEM((NB, COLS), bf16),
        pltpu.VMEM((NB, COLS), bf16),
    ]
    edges = [
        pltpu.VMEM((LB, PAD, COLS), f32),
        pltpu.VMEM((PAD, 8, COLS), f32),
        pltpu.VMEM((8, COLS), i32),
        pltpu.VMEM((8, COLS), i32),
    ]

    def finish(packed):
        return pl.pallas_call(
            finish_kernel,
            out_shape=shape,
            in_specs=[vmem],
            out_specs=anym,
            scratch_shapes=[dma((8,))],
            compiler_params=pltpu.CompilerParams(vmem_limit_bytes=16 * 2**20),
        )(packed)

    def whole(args):
        return (pl.pallas_call(
            whole_kernel,
            out_shape=pltpu.VMEM((LB, ROWS, COLS), f32),
            in_specs=in_specs,
            out_specs=vmem,
            scratch_shapes=edges + [
                pltpu.VMEM((ROWS, LB, COLS), f32),
                pltpu.VMEM((ROUNDS, NB, COLS), f32),
                pltpu.VMEM((ROUNDS, NB, COLS), f32),
                pltpu.VMEM((ROWS * LB, COLS), f32),
            ] + weights + [
                dma((10,)), dma((4,)), dma((4,)), dma((2, ROUNDS)),
                dma((ROUNDS, PEERS)), dma((ROUNDS, PEERS)), dma((ROUNDS, PEERS)), dma((ROUNDS, PEERS)),
            ],
            compiler_params=pltpu.CompilerParams(collective_id=1, has_side_effects=True, vmem_limit_bytes=58 * 2**20),
        )(*args[1:]))

    packed, flag = pl.pallas_call(
        sea_kernel,
        out_shape=(pltpu.VMEM((LB, ROWS, COLS), f32), pltpu.VMEM((8, COLS), f32)),
        in_specs=in_specs,
        out_specs=(vmem, vmem),
        scratch_shapes=edges + [
            pltpu.VMEM((TILES, LB, COLS), f32),
            pltpu.VMEM((EXT, LB, COLS), f32),
            pltpu.VMEM((2 * LB, EXT * COLS), bf16),
            pltpu.VMEM((TILES, EXT * COLS, COLS), bf16),
            pltpu.VMEM((16, COLS), f32),
            pltpu.VMEM((7, NB, COLS), f32),
            pltpu.VMEM((7, NB, COLS), f32),
            pltpu.VMEM((ROWS * LB, COLS), f32),
            pltpu.VMEM((2 * LB, EXT * COLS), f32),
        ] + weights + [
            pltpu.VMEM((4, 8, COLS), f32),
            pltpu.VMEM((4, 8, COLS), f32),
            dma((10,)), dma((4,)), dma((4,)),
            dma((TILES,)), dma((7, PEERS)), dma((7, PEERS)), dma((TILES,)),
            dma((2, 4)), dma((2, 4)),
        ],
        compiler_params=pltpu.CompilerParams(collective_id=0, has_side_effects=True, vmem_limit_bytes=58 * 2**20),
    )(*operands)
    return lax.cond(flag[0, 0] > 0.0, whole, lambda args: args[0], (packed,) + operands)


def solution(mesh):
    in_specs = (P("bins", "space", None), P("space", None), P(), P(), P(), P())
    out_specs = P("bins", "space", None)
    return jax.shard_map(local, mesh=mesh, in_specs=in_specs, out_specs=out_specs, check_vma=False)
```

```python
import functools
import math

import jax
import jax.numpy as jnp
import numpy as np
from jax import lax
from jax.experimental import pallas as pl
from jax.experimental.pallas import tpu as pltpu
from jax.sharding import PartitionSpec as P

NF = 32
ND = 36
SUBSTEPS = 4
PEERS = 8
SLABS = 16
LB = 144
NB = 1152
ROWS = 64
COLS = 128
PAD = ROWS + 16
ROUNDS = 8
MESH = pl.DeviceIdType.MESH


def device_of(slot):
    return (slot % 4) * 2 + slot // 4


def slot_of(device):
    return device // 2 + 4 * lax.rem(device, 2)


def advance(field, b0, me, cosv, sinv, lane, sub, sea):
    b = sub + b0
    one = lambda c: c.astype(jnp.float32)
    freq = (4 * me).astype(jnp.float32) + one(b >= ND) + one(b >= 2 * ND) + one(b >= 3 * ND)
    group = 0.9 / (1.0 + 2.3 * freq / max(NF - 1, 1))
    cx = group * cosv[pl.ds(b0, 8), :]
    cy = group * sinv[pl.ds(b0, 8), :]
    right, ahead = cx > 0.0, cy > 0.0
    ax, ay = jnp.abs(cx), jnp.abs(cy)
    stay = 1.0 - ay
    move = jnp.where((ahead & (lane == 0)) | (~ahead & (lane == COLS - 1)), 0.0, ay)
    for step in range(SUBSTEPS):
        n = field.shape[0] - 2
        mid = field[1:-1]
        near = jnp.where(right[None], field[:-2], field[2:])
        mid = mid + ax[None] * (near - mid)
        near = jnp.stack([jnp.where(ahead, pltpu.roll(mid[i], 1, 1), pltpu.roll(mid[i], COLS - 1, 1)) for i in range(n)])
        field = (stay[None] * mid + move[None] * near) * sea(step, n)
    return field


def whole_kernel(x, mask, cosv, sinv, grow, band, kg, kl, out,
           fin, seab, mlo, mhi, sent, got, fresh, back, kgv, klv, growb, bandb, state, square,
           load_sem, halo_send, halo_recv, own_sem, fs, fr, bs, br):
    me = lax.axis_index("bins")
    space = lax.axis_index("space")
    up = lax.rem(space + 1, SLABS)
    down = lax.rem(space + SLABS - 1, SLABS)

    barrier = pltpu.get_barrier_semaphore()
    for i in range(1, PEERS):
        pl.semaphore_signal(barrier, inc=1, device_id=(lax.rem(me + i, PEERS), space), device_id_type=MESH)
    for other in (up, down):
        pl.semaphore_signal(barrier, inc=1, device_id=(me, other), device_id_type=MESH)

    def load(q):
        return pltpu.make_async_copy(x.at[:, pl.ds(8 * q, 8), :], fin.at[:, pl.ds(8 * q + 8, 8), :], load_sem.at[q])

    for q in (1, 2, 3, 4, 5, 6, 0, 7):
        load(q).start()
    weights = [pltpu.make_async_copy(kg, kgv, load_sem.at[8]), pltpu.make_async_copy(kl, klv, load_sem.at[9])]

    for q in range(ROWS // 8):
        sea = mask[8 * q:8 * q + 8, :].astype(jnp.float32)
        for i in range(8):
            seab[8 + 8 * q + i] = jnp.broadcast_to(sea[i:i + 1, :], (8, COLS))

    halos = [
        pltpu.make_async_remote_copy(x.at[:, pl.ds(56, 8), :], fin.at[:, pl.ds(0, 8), :], halo_send.at[0], halo_recv.at[0],
                                     device_id=(me, up), device_id_type=MESH),
        pltpu.make_async_remote_copy(x.at[:, pl.ds(0, 8), :], fin.at[:, pl.ds(72, 8), :], halo_send.at[1], halo_recv.at[1],
                                     device_id=(me, down), device_id_type=MESH),
        pltpu.make_async_remote_copy(mask.at[pl.ds(56, 8), :], mlo, halo_send.at[2], halo_recv.at[2],
                                     device_id=(me, up), device_id_type=MESH),
        pltpu.make_async_remote_copy(mask.at[pl.ds(0, 8), :], mhi, halo_send.at[3], halo_recv.at[3],
                                     device_id=(me, down), device_id_type=MESH),
    ]
    inside_lo = (space > 0).astype(jnp.float32)
    inside_hi = (space < SLABS - 1).astype(jnp.float32)
    flat = fin.reshape(LB * PAD, COLS)
    lane = lax.broadcasted_iota(jnp.int32, (8, COLS), 1)
    sub = lax.broadcasted_iota(jnp.int32, (8, COLS), 0)

    def propagate(g):
        def tile(t, carry):
            b0 = pl.multiple_of(t * 8, 8)
            rows = [flat[pl.ds(b0 * PAD + 16 * g + 4 + i, 8, stride=PAD), :] for i in range(24)]
            if g == 0:
                rows = [r * inside_lo for r in rows[:4]] + rows[4:]
            if g == 3:
                rows = rows[:20] + [r * inside_hi for r in rows[20:]]
            field = jnp.stack(rows)
            field = advance(field, b0, me, cosv, sinv, lane, sub, lambda step, n: seab[pl.ds(16 * g + 5 + step, n)])
            sent[pl.ds(16 * g, 16), pl.ds(b0, 8), :] = field
            return carry
        lax.fori_loop(0, LB // 8, tile, 0, unroll=2)

    def forward(j, d):
        row = 8 * j + slot_of(d)
        return pltpu.make_async_remote_copy(
            sent.at[row], got.at[j, pl.ds(me * LB, LB), :], fs.at[j, d], fr.at[j, me],
            device_id=(d, space), device_id_type=MESH)

    def arrival(j, d):
        return pltpu.make_async_remote_copy(
            sent.at[0], got.at[j, pl.ds(d * LB, LB), :], fs.at[j, d], fr.at[j, d],
            device_id=(d, space), device_id_type=MESH)

    def own(j):
        return pltpu.make_async_copy(sent.at[8 * j + slot_of(me)], got.at[j, pl.ds(me * LB, LB), :], own_sem.at[0, j])

    def give(j, d):
        return pltpu.make_async_remote_copy(
            fresh.at[j, pl.ds(d * LB, LB), :], back.at[pl.ds((8 * j + slot_of(me)) * LB, LB), :], bs.at[j, d], br.at[j, me],
            device_id=(d, space), device_id_type=MESH)

    def returned(j, d):
        return pltpu.make_async_remote_copy(
            fresh.at[j, pl.ds(d * LB, LB), :], back.at[pl.ds((8 * j + slot_of(d)) * LB, LB), :], bs.at[j, d], br.at[j, d],
            device_id=(d, space), device_id_type=MESH)

    def keep(j):
        return pltpu.make_async_copy(
            fresh.at[j, pl.ds(me * LB, LB), :], back.at[pl.ds((8 * j + slot_of(me)) * LB, LB), :], own_sem.at[1, j])

    def others(body):
        def step(i, carry):
            body(lax.rem(me + i, PEERS))
            return carry
        lax.fori_loop(1, PEERS, step, 0)

    ready = set()
    first = True
    for g in (1, 2, 0, 3):
        for q in range(max(2 * g - 1, 0), min(2 * g + 3, 8)):
            if q not in ready:
                load(q).wait()
                ready.add(q)
        if g == 0:
            for h in halos:
                h.wait_recv()
            for q, (ref, inside) in ((0, (mlo, inside_lo)), (72, (mhi, inside_hi))):
                sea = ref[...].astype(jnp.float32) * inside
                for i in range(8):
                    seab[q + i] = jnp.broadcast_to(sea[i:i + 1, :], (8, COLS))
        propagate(g)
        if first:
            pl.semaphore_wait(barrier, PEERS + 1)
            for h in halos:
                h.start()
            first = False
        for j in (2 * g, 2 * g + 1):
            others(lambda d: forward(j, d).start())
            own(j).start()
        if g == 2:
            for w in weights:
                w.start()
            for i in range(NB // COLS):
                at = pl.ds(i * COLS, COLS)
                growb[at, :] = jnp.transpose(jnp.broadcast_to(0.25 * grow[i:i + 1, :] + 1.0, (COLS, COLS)))
                bandb[at, :] = jnp.transpose(jnp.broadcast_to(band[i:i + 1, :], (COLS, COLS)))
    for w in weights:
        w.wait()

    order = (2, 3, 4, 5, 0, 1, 6, 7)

    def sources(j):
        others(lambda d: arrival(j, d).wait_recv())
        own(j).wait()

        def prepare(i, total):
            at = pl.ds(pl.multiple_of(i * LB, LB), LB)
            field = got[j, at, :]
            state[at, :] = field.astype(jnp.bfloat16)
            square[at, :] = (field * field).astype(jnp.bfloat16)
            return total + jnp.sum((bandb[at, :] * field).reshape(LB // 8, 8, COLS), axis=0)
        energy = jnp.sum(lax.fori_loop(0, PEERS, prepare, jnp.zeros((8, COLS), jnp.float32)), axis=0, keepdims=True)
        damp = 1.0 / (1.0 + 0.5 * energy)

        def owner(i, carry):
            d = lax.rem(me + i, PEERS)
            at = pl.ds(pl.multiple_of(d * LB, LB), LB)
            gain = jnp.dot(kgv[at, :], state[...], preferred_element_type=jnp.float32)
            loss = jnp.dot(klv[at, :], square[...], preferred_element_type=jnp.float32)
            field = got[j, at, :]
            fresh[j, at, :] = (field * (growb[at, :] + 0.25 * gain) - 0.25 * loss) * damp

            @pl.when(i < PEERS)
            def _():
                give(j, d).start()
            return carry
        lax.fori_loop(1, PEERS + 1, owner, 0)
        keep(j).start()

    for j in order:
        sources(j)

    for j in order:
        others(lambda d: returned(j, d).wait_recv())
        keep(j).wait()
        sea = mask[8 * j:8 * j + 8, :].astype(jnp.float32)

        def turn(b, carry):
            out[b, pl.ds(8 * j, 8), :] = back[pl.ds(8 * j * LB + b, 8, stride=LB), :] * sea
            return carry
        lax.fori_loop(0, LB, turn, 0, unroll=8)

    for h in halos:
        h.wait_send()
    for j in order:
        others(lambda d: forward(j, d).wait_send())
        others(lambda d: give(j, d).wait_send())


ORDER = (1, 2, 0, 3)
BASE = 13
EXT = 3
TILES = BASE * 4
SPLIT = 80


def sea_kernel(x, mask_at, cos_at, sin_at, grow_at, band_at, kg, kl, out, flag,
               fin, seab, mlo, mhi, sent, extra, halves, place, hole_at, got, fresh, back, total,
               kgv, klv, growb, bandb, state, square, flx, flz,
               load_sem, halo_send, halo_recv, fs, fr, bs, br, fls, flr, first_sem,
               mask, cosv, sinv, grow, band, small_sem):
    me = lax.axis_index("bins")
    space = lax.axis_index("space")
    up = lax.rem(space + 1, SLABS)
    down = lax.rem(space + SLABS - 1, SLABS)
    core = lax.rem(me, 2)
    mine = slot_of(me)
    sx = lax.rem(space, 4)
    sz = space // 4
    f32, bf16 = jnp.float32, jnp.bfloat16

    def x_peer(i):
        return sz * 4 + lax.rem(sx + i, 4)

    def z_peer(i):
        return lax.rem(sz + i, 4) * 4 + sx

    barrier = pltpu.get_barrier_semaphore()
    for i in range(1, PEERS):
        pl.semaphore_signal(barrier, inc=1, device_id=(lax.rem(me + i, PEERS), space), device_id_type=MESH)
    for other in [up, down] + [x_peer(i) for i in (1, 2, 3)] + [z_peer(i) for i in (1, 2, 3)]:
        pl.semaphore_signal(barrier, inc=1, device_id=(me, other), device_id_type=MESH)

    small = [pltpu.make_async_copy(source, target, small_sem.at[i]) for i, (source, target) in enumerate(
        ((mask_at, mask), (cos_at, cosv), (sin_at, sinv), (grow_at, grow), (band_at, band)))]
    for copy in small:
        copy.start()

    def load(q):
        return pltpu.make_async_copy(x.at[:, pl.ds(8 * q, 8), :], fin.at[:, pl.ds(8 * q + 8, 8), :], load_sem.at[q])

    def load_part(q, lo, hi):
        return pltpu.make_async_copy(x.at[pl.ds(lo, hi - lo), pl.ds(8 * q, 8), :], fin.at[pl.ds(lo, hi - lo), pl.ds(8 * q + 8, 8), :],
                                     load_sem.at[q] if lo else first_sem.at[q])

    for lo, hi in ((0, SPLIT), (SPLIT, LB)):
        for q in (1, 2, 3, 4):
            load_part(q, lo, hi).start()
    for q in (5, 6, 0, 7):
        load(q).start()
    weights = [pltpu.make_async_copy(kg, kgv, load_sem.at[8]), pltpu.make_async_copy(kl, klv, load_sem.at[9])]

    small[0].wait()
    for q in range(ROWS // 8):
        sea = mask[8 * q:8 * q + 8, :].astype(f32)
        for i in range(8):
            seab[8 + 8 * q + i] = jnp.broadcast_to(sea[i:i + 1, :], (8, COLS))

    halos = [
        pltpu.make_async_remote_copy(x.at[:, pl.ds(60, 4), :], fin.at[:, pl.ds(4, 4), :], halo_send.at[0], halo_recv.at[0],
                                     device_id=(me, up), device_id_type=MESH),
        pltpu.make_async_remote_copy(x.at[:, pl.ds(0, 4), :], fin.at[:, pl.ds(72, 4), :], halo_send.at[1], halo_recv.at[1],
                                     device_id=(me, down), device_id_type=MESH),
        pltpu.make_async_remote_copy(mask_at.at[pl.ds(56, 8), :], mlo, halo_send.at[2], halo_recv.at[2],
                                     device_id=(me, up), device_id_type=MESH),
        pltpu.make_async_remote_copy(mask_at.at[pl.ds(0, 8), :], mhi, halo_send.at[3], halo_recv.at[3],
                                     device_id=(me, down), device_id_type=MESH),
    ]
    inside_lo = (space > 0).astype(f32)
    inside_hi = (space < SLABS - 1).astype(f32)
    flat = fin.reshape(LB * PAD, COLS)
    lane = lax.broadcasted_iota(jnp.int32, (8, COLS), 1)
    sub = lax.broadcasted_iota(jnp.int32, (8, COLS), 0)

    before = (lax.broadcasted_iota(jnp.int32, (COLS, COLS), 0) < lax.broadcasted_iota(jnp.int32, (COLS, COLS), 1)).astype(f32).astype(bf16)
    ones = jnp.ones((COLS, COLS), bf16)

    def assign(p):
        g = ORDER[p]
        sea = mask[16 * g:16 * g + 16, :].astype(f32)
        row = lax.broadcasted_iota(jnp.int32, (16, COLS), 0)
        pick = jnp.where(row < BASE, 1.0 - sea, sea)
        ranks = jnp.dot(pick.astype(bf16), before, preferred_element_type=f32)
        counts = jnp.dot(pick.astype(bf16), ones, preferred_element_type=f32)
        holes = jnp.zeros((1, COLS), f32)
        for i in range(BASE):
            hole_at[i:i + 1, :] = jnp.where(pick[i:i + 1] > 0.0, ranks[i:i + 1] + holes, -1.0)
            holes = holes + counts[i:i + 1]
        filled = jnp.zeros((1, COLS), f32)
        wants = []
        for i in range(BASE, 16):
            want = jnp.where(pick[i:i + 1] > 0.0, ranks[i:i + 1] + filled, -2.0)
            wants.append(jnp.transpose(jnp.broadcast_to(want, (COLS, COLS))))
            filled = filled + counts[i:i + 1]

        def one(i, carry):
            hole = hole_at[pl.ds(i, 1), :]
            for k in range(EXT):
                place[BASE * p + i, k * COLS:(k + 1) * COLS, :] = jnp.where(wants[k] == hole, 1.0, 0.0).astype(bf16)
            return carry
        lax.fori_loop(0, BASE, one, 0)
        return filled - holes

    def propagate(p, lo, hi):
        g = ORDER[p]

        def tile(t, carry):
            b0 = pl.multiple_of(lo + t * 8, 8)
            rows = [flat[pl.ds(b0 * PAD + 16 * g + 4 + i, 8, stride=PAD), :] for i in range(24)]
            if g == 0:
                rows = [r * inside_lo for r in rows[:4]] + rows[4:]
            if g == 3:
                rows = rows[:20] + [r * inside_hi for r in rows[20:]]
            field = advance(jnp.stack(rows), b0, me, cosv, sinv, lane, sub, lambda step, n: seab[pl.ds(16 * g + 5 + step, n)])
            sent[pl.ds(BASE * p, BASE), pl.ds(b0, 8), :] = field[:BASE]
            extra[:, pl.ds(b0, 8), :] = field[BASE:]
            return carry
        lax.fori_loop(0, (hi - lo) // 8, tile, 0, unroll=2)
        for k in range(EXT):
            cells = extra[k, lo:hi, :]
            high = cells.astype(bf16)
            halves[2 * lo:lo + hi, k * COLS:(k + 1) * COLS] = high
            halves[lo + hi:2 * hi, k * COLS:(k + 1) * COLS] = (cells - high.astype(f32)).astype(bf16)

    def forward(q, lo=0, hi=LB):
        d = device_of(lax.rem(q, 8))
        return d, pltpu.make_async_remote_copy(
            sent.at[q, pl.ds(lo, hi - lo), :], got.at[q // 8, pl.ds(me * LB + lo, hi - lo), :], fs.at[q], fr.at[q // 8, me],
            device_id=(d, space), device_id_type=MESH)

    def arrival(j, d):
        return pltpu.make_async_remote_copy(
            sent.at[0], got.at[j, pl.ds(d * LB, LB), :], fs.at[0], fr.at[j, d],
            device_id=(lax.rem(me + 1, PEERS), space), device_id_type=MESH)

    def seat(q):
        return ((q // BASE) * 16 + lax.rem(q, BASE)) * LB

    def give(j, d):
        return pltpu.make_async_remote_copy(
            fresh.at[j, pl.ds(d * LB, LB), :], back.at[pl.ds(seat(8 * j + mine), LB), :], bs.at[j, d], br.at[8 * j + mine],
            device_id=(d, space), device_id_type=MESH)

    def returned(q):
        return pltpu.make_async_remote_copy(
            fresh.at[0, pl.ds(0, LB), :], back.at[pl.ds(seat(q), LB), :], bs.at[0, 0], br.at[q],
            device_id=(lax.rem(me + 1, PEERS), space), device_id_type=MESH)

    def fill_and_send(p, lo, hi):
        n = hi - lo
        at = pl.ds(lo, n)

        def one(i, carry):
            q = BASE * p + i
            moved = jnp.dot(halves[2 * lo:2 * hi, :], place[q], preferred_element_type=f32)
            sent[q, at, :] = sent[q, at, :] + (moved[:n] + moved[n:])
            d, copy = forward(q, lo, hi)

            @pl.when(d != me)
            def _():
                copy.start()

            @pl.when(d == me)
            def _():
                pltpu.make_async_copy(sent.at[q, at, :], got.at[q // 8, pl.ds(me * LB + lo, n), :], fr.at[q // 8, me]).start()
            return carry
        lax.fori_loop(0, BASE, one, 0)

    ready = set()
    over = assign(0)
    for copy in small[1:]:
        copy.wait()
    for p, g in enumerate(ORDER):
        for q in range(max(2 * g - 1, 0), min(2 * g + 3, 8)):
            if q not in ready and p > 0:
                load(q).wait()
            ready.add(q)
        if p == 2:
            for h in halos:
                h.wait_recv()
            for q, (ref, inside) in ((0, (mlo, inside_lo)), (72, (mhi, inside_hi))):
                sea = ref[...].astype(f32) * inside
                for i in range(8):
                    seab[q + i] = jnp.broadcast_to(sea[i:i + 1, :], (8, COLS))
        for lo, hi in ((0, SPLIT), (SPLIT, LB)) if p == 0 else ((0, LB),):
            if p == 0:
                for q in (1, 2, 3, 4):
                    load_part(q, lo, hi).wait()
            propagate(p, lo, hi)
            if p == 0 and lo == 0:
                pl.semaphore_wait(barrier, PEERS + 7)
                for h in halos:
                    h.start()
            fill_and_send(p, lo, hi)
        if p < 3:
            over = jnp.maximum(over, assign(p + 1))
        if p == 1:
            for w in weights:
                w.start()
            for i in range(NB // COLS):
                at = pl.ds(i * COLS, COLS)
                growb[at, :] = jnp.transpose(jnp.broadcast_to(0.25 * grow[i:i + 1, :] + 1.0, (COLS, COLS)))
                bandb[at, :] = jnp.transpose(jnp.broadcast_to(band[i:i + 1, :], (COLS, COLS)))

    def tell(stage, i):
        ref, at, to = ((flx, sx, x_peer(i)), (flz, sz, z_peer(i)))[stage]
        return pltpu.make_async_remote_copy(ref.at[at], ref.at[at], fls.at[stage, i], flr.at[stage, at],
                                            device_id=(me, to), device_id_type=MESH)

    def told(stage, i):
        ref, at, to = ((flx, sx, x_peer(i)), (flz, sz, z_peer(i)))[stage]
        at = lax.rem(at + i, 4)
        return pltpu.make_async_remote_copy(ref.at[at], ref.at[at], fls.at[stage, i], flr.at[stage, at],
                                            device_id=(me, to), device_id_type=MESH)

    flx[sx] = jnp.broadcast_to(over, (8, COLS))
    for i in (1, 2, 3):
        tell(0, i).start()
    for w in weights:
        w.wait()

    def sources(j):
        def each(d, carry):
            arrival(j, d).wait_recv()
            return carry
        lax.fori_loop(0, PEERS, each, 0)

        def prepare(i, total):
            at = pl.ds(pl.multiple_of(i * LB, LB), LB)
            field = got[j, at, :]
            state[at, :] = field.astype(bf16)
            square[at, :] = (field * field).astype(bf16)
            return total + jnp.sum((bandb[at, :] * field).reshape(LB // 8, 8, COLS), axis=0)
        energy = jnp.sum(lax.fori_loop(0, PEERS, prepare, jnp.zeros((8, COLS), f32)), axis=0, keepdims=True)
        damp = 1.0 / (1.0 + 0.5 * energy)

        def owner(i, carry):
            d = lax.rem(me + i, PEERS)
            at = pl.ds(pl.multiple_of(d * LB, LB), LB)
            gain = jnp.dot(kgv[at, :], state[...], preferred_element_type=f32)
            loss = jnp.dot(klv[at, :], square[...], preferred_element_type=f32)
            field = got[j, at, :]
            fresh[j, at, :] = (field * (growb[at, :] + 0.25 * gain) - 0.25 * loss) * damp

            @pl.when(i < PEERS)
            def _():
                give(j, d).start()
            return carry
        lax.fori_loop(1, PEERS + 1, owner, 0)
        pltpu.make_async_copy(
            fresh.at[j, pl.ds(me * LB, LB), :], back.at[pl.ds(seat(8 * j + mine), LB), :], br.at[8 * j + mine]).start()

    def full_rounds(j, carry):
        sources(j)
        return carry
    lax.fori_loop(0, 6, full_rounds, 0)

    @pl.when(core == 0)
    def _():
        sources(6)

    for i in (1, 2, 3):
        told(0, i).wait_recv()
    flz[sz] = jnp.maximum(jnp.maximum(flx[0], flx[1]), jnp.maximum(flx[2], flx[3]))
    for i in (1, 2, 3):
        tell(1, i).start()

    for p, g in enumerate(ORDER):
        total[...] = jnp.zeros_like(total)

        def pull(i, carry):
            q = BASE * p + i
            returned(q).wait_recv()
            cells = back[pl.ds(pl.multiple_of((16 * p + i) * LB, LB), LB), :]
            high = cells.astype(bf16)
            low = (cells - high.astype(f32)).astype(bf16)
            both = jnp.concatenate([high, low], axis=0)
            total[...] += lax.dot_general(both, place[q], (((1,), (1,)), ((), ())), preferred_element_type=f32)
            return carry
        lax.fori_loop(0, BASE, pull, 0)
        for k in range(EXT):
            at = slice(k * COLS, (k + 1) * COLS)
            back[pl.ds((16 * p + BASE + k) * LB, LB), :] = total[:LB, at] + total[LB:, at]
        for h in (0, 1):
            r0 = 16 * g + 8 * h
            sea = mask[r0:r0 + 8, :].astype(f32)

            def turn(b, carry):
                out[b, pl.ds(r0, 8), :] = back[pl.ds((16 * p + 8 * h) * LB + b, 8, stride=LB), :] * sea
                return carry
            lax.fori_loop(0, LB, turn, 0, unroll=8)

    for i in (1, 2, 3):
        told(1, i).wait_recv()
    flag[...] = jnp.maximum(jnp.maximum(flz[0], flz[1]), jnp.maximum(flz[2], flz[3]))
    for h in halos:
        h.wait_send()
    for i in (1, 2, 3):
        tell(0, i).wait_send()
        tell(1, i).wait_send()

    def drain(q, carry):
        d, copy = forward(q)

        @pl.when(d != me)
        def _():
            copy.wait_send()
        return carry
    lax.fori_loop(0, TILES, drain, 0)

    def drain_round(j):
        def step(i, carry):
            give(j, lax.rem(me + i, PEERS)).wait_send()
            return carry
        lax.fori_loop(1, PEERS, step, 0)

    for j in range(6):
        drain_round(j)

    @pl.when(core == 0)
    def _():
        drain_round(6)


def finish_kernel(packed, out, sems):
    part = LB // 8
    copies = [pltpu.make_async_copy(packed.at[pl.ds(i * part, part)], out.at[pl.ds(i * part, part)], sems.at[i]) for i in range(8)]
    for copy in copies:
        copy.start()
    for copy in copies:
        copy.wait()


def local(spectra, land_mask, growth, band_weight, kernel_gain, kernel_loss):
    theta = 2.0 * math.pi * (np.arange(LB) % ND + 0.5) / ND
    wide = lambda v: jnp.asarray(np.repeat(v.astype(np.float32)[:, None], COLS, 1))
    vmem = pl.BlockSpec(memory_space=pltpu.VMEM)
    anym = pl.BlockSpec(memory_space=pl.ANY)
    f32, bf16, i32 = jnp.float32, jnp.bfloat16, jnp.int32
    dma = pltpu.SemaphoreType.DMA
    shape = jax.ShapeDtypeStruct((LB, ROWS, COLS), f32)
    operands = (spectra, land_mask, wide(np.cos(theta)), wide(np.sin(theta)),
                growth.reshape(NB // COLS, COLS), band_weight.reshape(NB // COLS, COLS), kernel_gain, kernel_loss)
    in_specs = [anym, vmem, vmem, vmem, vmem, vmem, anym, anym]
    weights = [
        pltpu.VMEM((NB, NB), bf16),
        pltpu.VMEM((NB, NB), bf16),
        pltpu.VMEM((NB, COLS), f32),
        pltpu.VMEM((NB, COLS), f32),
        pltpu.VMEM((NB, COLS), bf16),
        pltpu.VMEM((NB, COLS), bf16),
    ]
    edges = [
        pltpu.VMEM((LB, PAD, COLS), f32),
        pltpu.VMEM((PAD, 8, COLS), f32),
        pltpu.VMEM((8, COLS), i32),
        pltpu.VMEM((8, COLS), i32),
    ]

    def finish(packed):
        return pl.pallas_call(
            finish_kernel,
            out_shape=shape,
            in_specs=[vmem],
            out_specs=anym,
            scratch_shapes=[dma((8,))],
            compiler_params=pltpu.CompilerParams(vmem_limit_bytes=16 * 2**20),
        )(packed)

    def whole(args):
        return (pl.pallas_call(
            whole_kernel,
            out_shape=pltpu.VMEM((LB, ROWS, COLS), f32),
            in_specs=in_specs,
            out_specs=vmem,
            scratch_shapes=edges + [
                pltpu.VMEM((ROWS, LB, COLS), f32),
                pltpu.VMEM((ROUNDS, NB, COLS), f32),
                pltpu.VMEM((ROUNDS, NB, COLS), f32),
                pltpu.VMEM((ROWS * LB, COLS), f32),
            ] + weights + [
                dma((10,)), dma((4,)), dma((4,)), dma((2, ROUNDS)),
                dma((ROUNDS, PEERS)), dma((ROUNDS, PEERS)), dma((ROUNDS, PEERS)), dma((ROUNDS, PEERS)),
            ],
            compiler_params=pltpu.CompilerParams(collective_id=1, has_side_effects=True, vmem_limit_bytes=58 * 2**20),
        )(*args[1:]))

    packed, flag = pl.pallas_call(
        sea_kernel,
        out_shape=(pltpu.VMEM((LB, ROWS, COLS), f32), pltpu.VMEM((8, COLS), f32)),
        in_specs=[anym] * 8,
        out_specs=(vmem, vmem),
        scratch_shapes=edges + [
            pltpu.VMEM((TILES, LB, COLS), f32),
            pltpu.VMEM((EXT, LB, COLS), f32),
            pltpu.VMEM((2 * LB, EXT * COLS), bf16),
            pltpu.VMEM((TILES, EXT * COLS, COLS), bf16),
            pltpu.VMEM((16, COLS), f32),
            pltpu.VMEM((7, NB, COLS), f32),
            pltpu.VMEM((7, NB, COLS), f32),
            pltpu.VMEM((ROWS * LB, COLS), f32),
            pltpu.VMEM((2 * LB, EXT * COLS), f32),
        ] + weights + [
            pltpu.VMEM((4, 8, COLS), f32),
            pltpu.VMEM((4, 8, COLS), f32),
            dma((10,)), dma((4,)), dma((4,)),
            dma((TILES,)), dma((7, PEERS)), dma((7, PEERS)), dma((TILES,)),
            dma((2, 4)), dma((2, 4)), dma((8,)),
            pltpu.VMEM((ROWS, COLS), i32),
            pltpu.VMEM((LB, COLS), f32),
            pltpu.VMEM((LB, COLS), f32),
            pltpu.VMEM((NB // COLS, COLS), f32),
            pltpu.VMEM((NB // COLS, COLS), f32),
            dma((5,)),
        ],
        compiler_params=pltpu.CompilerParams(collective_id=0, has_side_effects=True, vmem_limit_bytes=58 * 2**20),
    )(*operands)
    return lax.cond(flag[0, 0] > 0.0, whole, lambda args: args[0], (packed,) + operands)


def solution(mesh):
    in_specs = (P("bins", "space", None), P("space", None), P(), P(), P(), P())
    out_specs = P("bins", "space", None)
    return jax.shard_map(local, mesh=mesh, in_specs=in_specs, out_specs=out_specs, check_vma=False)
```

```python
import functools
import math

import jax
import jax.numpy as jnp
import numpy as np
from jax import lax
from jax.experimental import pallas as pl
from jax.experimental.pallas import tpu as pltpu
from jax.sharding import PartitionSpec as P

NF = 32
ND = 36
SUBSTEPS = 4
PEERS = 8
SLABS = 16
LB = 144
NB = 1152
ROWS = 64
COLS = 128
PAD = ROWS + 16
ROUNDS = 8
MESH = pl.DeviceIdType.MESH


def device_of(slot):
    return (slot % 4) * 2 + slot // 4


def slot_of(device):
    return device // 2 + 4 * lax.rem(device, 2)


def advance(field, b0, me, cosv, sinv, lane, sub, sea):
    b = sub + b0
    one = lambda c: c.astype(jnp.float32)
    freq = (4 * me).astype(jnp.float32) + one(b >= ND) + one(b >= 2 * ND) + one(b >= 3 * ND)
    group = 0.9 / (1.0 + 2.3 * freq / max(NF - 1, 1))
    cx = group * cosv[pl.ds(b0, 8), :]
    cy = group * sinv[pl.ds(b0, 8), :]
    right, ahead = cx > 0.0, cy > 0.0
    ax, ay = jnp.abs(cx), jnp.abs(cy)
    stay = 1.0 - ay
    move = jnp.where((ahead & (lane == 0)) | (~ahead & (lane == COLS - 1)), 0.0, ay)
    for step in range(SUBSTEPS):
        n = field.shape[0] - 2
        mid = field[1:-1]
        near = jnp.where(right[None], field[:-2], field[2:])
        mid = mid + ax[None] * (near - mid)
        near = jnp.stack([jnp.where(ahead, pltpu.roll(mid[i], 1, 1), pltpu.roll(mid[i], COLS - 1, 1)) for i in range(n)])
        field = (stay[None] * mid + move[None] * near) * sea(step, n)
    return field


def whole_kernel(x, mask, cosv, sinv, grow, band, kg, kl, out,
           fin, seab, mlo, mhi, sent, got, fresh, back, kgv, klv, growb, bandb, state, square,
           load_sem, halo_send, halo_recv, own_sem, fs, fr, bs, br):
    me = lax.axis_index("bins")
    space = lax.axis_index("space")
    up = lax.rem(space + 1, SLABS)
    down = lax.rem(space + SLABS - 1, SLABS)

    barrier = pltpu.get_barrier_semaphore()
    for i in range(1, PEERS):
        pl.semaphore_signal(barrier, inc=1, device_id=(lax.rem(me + i, PEERS), space), device_id_type=MESH)
    for other in (up, down):
        pl.semaphore_signal(barrier, inc=1, device_id=(me, other), device_id_type=MESH)

    def load(q):
        return pltpu.make_async_copy(x.at[:, pl.ds(8 * q, 8), :], fin.at[:, pl.ds(8 * q + 8, 8), :], load_sem.at[q])

    for q in (1, 2, 3, 4, 5, 6, 0, 7):
        load(q).start()
    weights = [pltpu.make_async_copy(kg, kgv, load_sem.at[8]), pltpu.make_async_copy(kl, klv, load_sem.at[9])]

    for q in range(ROWS // 8):
        sea = mask[8 * q:8 * q + 8, :].astype(jnp.float32)
        for i in range(8):
            seab[8 + 8 * q + i] = jnp.broadcast_to(sea[i:i + 1, :], (8, COLS))

    halos = [
        pltpu.make_async_remote_copy(x.at[:, pl.ds(56, 8), :], fin.at[:, pl.ds(0, 8), :], halo_send.at[0], halo_recv.at[0],
                                     device_id=(me, up), device_id_type=MESH),
        pltpu.make_async_remote_copy(x.at[:, pl.ds(0, 8), :], fin.at[:, pl.ds(72, 8), :], halo_send.at[1], halo_recv.at[1],
                                     device_id=(me, down), device_id_type=MESH),
        pltpu.make_async_remote_copy(mask.at[pl.ds(56, 8), :], mlo, halo_send.at[2], halo_recv.at[2],
                                     device_id=(me, up), device_id_type=MESH),
        pltpu.make_async_remote_copy(mask.at[pl.ds(0, 8), :], mhi, halo_send.at[3], halo_recv.at[3],
                                     device_id=(me, down), device_id_type=MESH),
    ]
    inside_lo = (space > 0).astype(jnp.float32)
    inside_hi = (space < SLABS - 1).astype(jnp.float32)
    flat = fin.reshape(LB * PAD, COLS)
    lane = lax.broadcasted_iota(jnp.int32, (8, COLS), 1)
    sub = lax.broadcasted_iota(jnp.int32, (8, COLS), 0)

    def propagate(g):
        def tile(t, carry):
            b0 = pl.multiple_of(t * 8, 8)
            rows = [flat[pl.ds(b0 * PAD + 16 * g + 4 + i, 8, stride=PAD), :] for i in range(24)]
            if g == 0:
                rows = [r * inside_lo for r in rows[:4]] + rows[4:]
            if g == 3:
                rows = rows[:20] + [r * inside_hi for r in rows[20:]]
            field = jnp.stack(rows)
            field = advance(field, b0, me, cosv, sinv, lane, sub, lambda step, n: seab[pl.ds(16 * g + 5 + step, n)])
            sent[pl.ds(16 * g, 16), pl.ds(b0, 8), :] = field
            return carry
        lax.fori_loop(0, LB // 8, tile, 0, unroll=2)

    def forward(j, d):
        row = 8 * j + slot_of(d)
        return pltpu.make_async_remote_copy(
            sent.at[row], got.at[j, pl.ds(me * LB, LB), :], fs.at[j, d], fr.at[j, me],
            device_id=(d, space), device_id_type=MESH)

    def arrival(j, d):
        return pltpu.make_async_remote_copy(
            sent.at[0], got.at[j, pl.ds(d * LB, LB), :], fs.at[j, d], fr.at[j, d],
            device_id=(d, space), device_id_type=MESH)

    def own(j):
        return pltpu.make_async_copy(sent.at[8 * j + slot_of(me)], got.at[j, pl.ds(me * LB, LB), :], own_sem.at[0, j])

    def give(j, d):
        return pltpu.make_async_remote_copy(
            fresh.at[j, pl.ds(d * LB, LB), :], back.at[pl.ds((8 * j + slot_of(me)) * LB, LB), :], bs.at[j, d], br.at[j, me],
            device_id=(d, space), device_id_type=MESH)

    def returned(j, d):
        return pltpu.make_async_remote_copy(
            fresh.at[j, pl.ds(d * LB, LB), :], back.at[pl.ds((8 * j + slot_of(d)) * LB, LB), :], bs.at[j, d], br.at[j, d],
            device_id=(d, space), device_id_type=MESH)

    def keep(j):
        return pltpu.make_async_copy(
            fresh.at[j, pl.ds(me * LB, LB), :], back.at[pl.ds((8 * j + slot_of(me)) * LB, LB), :], own_sem.at[1, j])

    def others(body):
        def step(i, carry):
            body(lax.rem(me + i, PEERS))
            return carry
        lax.fori_loop(1, PEERS, step, 0)

    ready = set()
    first = True
    for g in (1, 2, 0, 3):
        for q in range(max(2 * g - 1, 0), min(2 * g + 3, 8)):
            if q not in ready:
                load(q).wait()
                ready.add(q)
        if g == 0:
            for h in halos:
                h.wait_recv()
            for q, (ref, inside) in ((0, (mlo, inside_lo)), (72, (mhi, inside_hi))):
                sea = ref[...].astype(jnp.float32) * inside
                for i in range(8):
                    seab[q + i] = jnp.broadcast_to(sea[i:i + 1, :], (8, COLS))
        propagate(g)
        if first:
            pl.semaphore_wait(barrier, PEERS + 1)
            for h in halos:
                h.start()
            first = False
        for j in (2 * g, 2 * g + 1):
            others(lambda d: forward(j, d).start())
            own(j).start()
        if g == 2:
            for w in weights:
                w.start()
            for i in range(NB // COLS):
                at = pl.ds(i * COLS, COLS)
                growb[at, :] = jnp.transpose(jnp.broadcast_to(0.25 * grow[i:i + 1, :] + 1.0, (COLS, COLS)))
                bandb[at, :] = jnp.transpose(jnp.broadcast_to(band[i:i + 1, :], (COLS, COLS)))
    for w in weights:
        w.wait()

    order = (2, 3, 4, 5, 0, 1, 6, 7)

    def sources(j):
        others(lambda d: arrival(j, d).wait_recv())
        own(j).wait()

        def prepare(i, total):
            at = pl.ds(pl.multiple_of(i * LB, LB), LB)
            field = got[j, at, :]
            state[at, :] = field.astype(jnp.bfloat16)
            square[at, :] = (field * field).astype(jnp.bfloat16)
            return total + jnp.sum((bandb[at, :] * field).reshape(LB // 8, 8, COLS), axis=0)
        energy = jnp.sum(lax.fori_loop(0, PEERS, prepare, jnp.zeros((8, COLS), jnp.float32)), axis=0, keepdims=True)
        damp = 1.0 / (1.0 + 0.5 * energy)

        def owner(i, carry):
            d = lax.rem(me + i, PEERS)
            at = pl.ds(pl.multiple_of(d * LB, LB), LB)
            gain = jnp.dot(kgv[at, :], state[...], preferred_element_type=jnp.float32)
            loss = jnp.dot(klv[at, :], square[...], preferred_element_type=jnp.float32)
            field = got[j, at, :]
            fresh[j, at, :] = (field * (growb[at, :] + 0.25 * gain) - 0.25 * loss) * damp

            @pl.when(i < PEERS)
            def _():
                give(j, d).start()
            return carry
        lax.fori_loop(1, PEERS + 1, owner, 0)
        keep(j).start()

    for j in order:
        sources(j)

    for j in order:
        others(lambda d: returned(j, d).wait_recv())
        keep(j).wait()
        sea = mask[8 * j:8 * j + 8, :].astype(jnp.float32)

        def turn(b, carry):
            out[b, pl.ds(8 * j, 8), :] = back[pl.ds(8 * j * LB + b, 8, stride=LB), :] * sea
            return carry
        lax.fori_loop(0, LB, turn, 0, unroll=8)

    for h in halos:
        h.wait_send()
    for j in order:
        others(lambda d: forward(j, d).wait_send())
        others(lambda d: give(j, d).wait_send())


ORDER = (1, 2, 0, 3)
BASE = 13
EXT = 3
TILES = BASE * 4
SPLIT = 96


def sea_kernel(x, mask_at, cos_at, sin_at, grow_at, band_at, kg, kl, out, flag,
               fin, seab, mlo, mhi, sent, extra, halves, place, hole_at, got, fresh, back, total,
               kgv, klv, growb, bandb, state, square, flx, flz,
               load_sem, halo_send, halo_recv, fs, fr, bs, br, fls, flr, first_sem,
               mask, cosv, sinv, grow, band, small_sem):
    me = lax.axis_index("bins")
    space = lax.axis_index("space")
    up = lax.rem(space + 1, SLABS)
    down = lax.rem(space + SLABS - 1, SLABS)
    core = lax.rem(me, 2)
    mine = slot_of(me)
    sx = lax.rem(space, 4)
    sz = space // 4
    f32, bf16 = jnp.float32, jnp.bfloat16

    def x_peer(i):
        return sz * 4 + lax.rem(sx + i, 4)

    def z_peer(i):
        return lax.rem(sz + i, 4) * 4 + sx

    barrier = pltpu.get_barrier_semaphore()
    for i in range(1, PEERS):
        pl.semaphore_signal(barrier, inc=1, device_id=(lax.rem(me + i, PEERS), space), device_id_type=MESH)
    for other in [up, down] + [x_peer(i) for i in (1, 2, 3)] + [z_peer(i) for i in (1, 2, 3)]:
        pl.semaphore_signal(barrier, inc=1, device_id=(me, other), device_id_type=MESH)

    small = [pltpu.make_async_copy(source, target, small_sem.at[i]) for i, (source, target) in enumerate(
        ((mask_at, mask), (cos_at, cosv), (sin_at, sinv), (grow_at, grow), (band_at, band)))]
    for copy in small:
        copy.start()

    def load(q):
        return pltpu.make_async_copy(x.at[:, pl.ds(8 * q, 8), :], fin.at[:, pl.ds(8 * q + 8, 8), :], load_sem.at[q])

    def load_part(q, lo, hi):
        return pltpu.make_async_copy(x.at[pl.ds(lo, hi - lo), pl.ds(8 * q, 8), :], fin.at[pl.ds(lo, hi - lo), pl.ds(8 * q + 8, 8), :],
                                     load_sem.at[q] if lo else first_sem.at[q])

    for lo, hi in ((0, SPLIT), (SPLIT, LB)):
        for q in (1, 2, 3, 4):
            load_part(q, lo, hi).start()
    for q in (5, 6, 0, 7):
        load(q).start()
    weights = [pltpu.make_async_copy(kg, kgv, load_sem.at[8]), pltpu.make_async_copy(kl, klv, load_sem.at[9])]

    small[0].wait()
    for q in range(ROWS // 8):
        sea = mask[8 * q:8 * q + 8, :].astype(f32)
        for i in range(8):
            seab[8 + 8 * q + i] = jnp.broadcast_to(sea[i:i + 1, :], (8, COLS))

    halos = [
        pltpu.make_async_remote_copy(x.at[:, pl.ds(60, 4), :], fin.at[:, pl.ds(4, 4), :], halo_send.at[0], halo_recv.at[0],
                                     device_id=(me, up), device_id_type=MESH),
        pltpu.make_async_remote_copy(x.at[:, pl.ds(0, 4), :], fin.at[:, pl.ds(72, 4), :], halo_send.at[1], halo_recv.at[1],
                                     device_id=(me, down), device_id_type=MESH),
        pltpu.make_async_remote_copy(mask_at.at[pl.ds(56, 8), :], mlo, halo_send.at[2], halo_recv.at[2],
                                     device_id=(me, up), device_id_type=MESH),
        pltpu.make_async_remote_copy(mask_at.at[pl.ds(0, 8), :], mhi, halo_send.at[3], halo_recv.at[3],
                                     device_id=(me, down), device_id_type=MESH),
    ]
    inside_lo = (space > 0).astype(f32)
    inside_hi = (space < SLABS - 1).astype(f32)
    flat = fin.reshape(LB * PAD, COLS)
    lane = lax.broadcasted_iota(jnp.int32, (8, COLS), 1)
    sub = lax.broadcasted_iota(jnp.int32, (8, COLS), 0)

    before = (lax.broadcasted_iota(jnp.int32, (COLS, COLS), 0) < lax.broadcasted_iota(jnp.int32, (COLS, COLS), 1)).astype(f32).astype(bf16)
    ones = jnp.ones((COLS, COLS), bf16)

    def assign(p):
        g = ORDER[p]
        sea = mask[16 * g:16 * g + 16, :].astype(f32)
        row = lax.broadcasted_iota(jnp.int32, (16, COLS), 0)
        pick = jnp.where(row < BASE, 1.0 - sea, sea)
        ranks = jnp.dot(pick.astype(bf16), before, preferred_element_type=f32)
        counts = jnp.dot(pick.astype(bf16), ones, preferred_element_type=f32)
        holes = jnp.zeros((1, COLS), f32)
        for i in range(BASE):
            hole_at[i:i + 1, :] = jnp.where(pick[i:i + 1] > 0.0, ranks[i:i + 1] + holes, -1.0)
            holes = holes + counts[i:i + 1]
        filled = jnp.zeros((1, COLS), f32)
        wants = []
        for i in range(BASE, 16):
            want = jnp.where(pick[i:i + 1] > 0.0, ranks[i:i + 1] + filled, -2.0)
            wants.append(jnp.transpose(jnp.broadcast_to(want, (COLS, COLS))))
            filled = filled + counts[i:i + 1]

        def one(i, carry):
            hole = hole_at[pl.ds(i, 1), :]
            for k in range(EXT):
                place[BASE * p + i, k * COLS:(k + 1) * COLS, :] = jnp.where(wants[k] == hole, 1.0, 0.0).astype(bf16)
            return carry
        lax.fori_loop(0, BASE, one, 0)
        return filled - holes

    def propagate(p, lo, hi):
        g = ORDER[p]

        def tile(t, carry):
            b0 = pl.multiple_of(lo + t * 8, 8)
            rows = [flat[pl.ds(b0 * PAD + 16 * g + 4 + i, 8, stride=PAD), :] for i in range(24)]
            if g == 0:
                rows = [r * inside_lo for r in rows[:4]] + rows[4:]
            if g == 3:
                rows = rows[:20] + [r * inside_hi for r in rows[20:]]
            field = advance(jnp.stack(rows), b0, me, cosv, sinv, lane, sub, lambda step, n: seab[pl.ds(16 * g + 5 + step, n)])
            sent[pl.ds(BASE * p, BASE), pl.ds(b0, 8), :] = field[:BASE]
            extra[:, pl.ds(b0, 8), :] = field[BASE:]
            return carry
        lax.fori_loop(0, (hi - lo) // 8, tile, 0, unroll=3)
        for k in range(EXT):
            cells = extra[k, lo:hi, :]
            high = cells.astype(bf16)
            halves[2 * lo:lo + hi, k * COLS:(k + 1) * COLS] = high
            halves[lo + hi:2 * hi, k * COLS:(k + 1) * COLS] = (cells - high.astype(f32)).astype(bf16)

    def forward(q, lo=0, hi=LB):
        d = device_of(lax.rem(q, 8))
        return d, pltpu.make_async_remote_copy(
            sent.at[q, pl.ds(lo, hi - lo), :], got.at[q // 8, pl.ds(me * LB + lo, hi - lo), :], fs.at[q], fr.at[q // 8, me],
            device_id=(d, space), device_id_type=MESH)

    def arrival(j, d):
        return pltpu.make_async_remote_copy(
            sent.at[0], got.at[j, pl.ds(d * LB, LB), :], fs.at[0], fr.at[j, d],
            device_id=(lax.rem(me + 1, PEERS), space), device_id_type=MESH)

    def seat(q):
        return ((q // BASE) * 16 + lax.rem(q, BASE)) * LB

    def give(j, d):
        return pltpu.make_async_remote_copy(
            fresh.at[j, pl.ds(d * LB, LB), :], back.at[pl.ds(seat(8 * j + mine), LB), :], bs.at[j, d], br.at[8 * j + mine],
            device_id=(d, space), device_id_type=MESH)

    def returned(q):
        return pltpu.make_async_remote_copy(
            fresh.at[0, pl.ds(0, LB), :], back.at[pl.ds(seat(q), LB), :], bs.at[0, 0], br.at[q],
            device_id=(lax.rem(me + 1, PEERS), space), device_id_type=MESH)

    def fill_and_send(p, lo, hi):
        n = hi - lo
        at = pl.ds(lo, n)

        def one(i, carry):
            q = BASE * p + i
            moved = jnp.dot(halves[2 * lo:2 * hi, :], place[q], preferred_element_type=f32)
            sent[q, at, :] = sent[q, at, :] + (moved[:n] + moved[n:])
            d, copy = forward(q, lo, hi)

            @pl.when(d != me)
            def _():
                copy.start()

            @pl.when(d == me)
            def _():
                pltpu.make_async_copy(sent.at[q, at, :], got.at[q // 8, pl.ds(me * LB + lo, n), :], fr.at[q // 8, me]).start()
            return carry
        lax.fori_loop(0, BASE, one, 0)

    ready = set()
    over = assign(0)
    for copy in small[1:]:
        copy.wait()
    for p, g in enumerate(ORDER):
        for q in range(max(2 * g - 1, 0), min(2 * g + 3, 8)):
            if q not in ready and p > 0:
                load(q).wait()
            ready.add(q)
        if p == 2:
            for h in halos:
                h.wait_recv()
            for q, (ref, inside) in ((0, (mlo, inside_lo)), (72, (mhi, inside_hi))):
                sea = ref[...].astype(f32) * inside
                for i in range(8):
                    seab[q + i] = jnp.broadcast_to(sea[i:i + 1, :], (8, COLS))
        for lo, hi in ((0, SPLIT), (SPLIT, LB)) if p == 0 else ((0, LB),):
            if p == 0:
                for q in (1, 2, 3, 4):
                    load_part(q, lo, hi).wait()
            propagate(p, lo, hi)
            if p == 0 and lo == 0:
                pl.semaphore_wait(barrier, PEERS + 7)
                for h in halos:
                    h.start()
            fill_and_send(p, lo, hi)
        if p < 3:
            over = jnp.maximum(over, assign(p + 1))
        if p == 1:
            for w in weights:
                w.start()
            for i in range(NB // COLS):
                at = pl.ds(i * COLS, COLS)
                growb[at, :] = jnp.transpose(jnp.broadcast_to(0.25 * grow[i:i + 1, :] + 1.0, (COLS, COLS)))
                bandb[at, :] = jnp.transpose(jnp.broadcast_to(band[i:i + 1, :], (COLS, COLS)))

    def tell(stage, i):
        ref, at, to = ((flx, sx, x_peer(i)), (flz, sz, z_peer(i)))[stage]
        return pltpu.make_async_remote_copy(ref.at[at], ref.at[at], fls.at[stage, i], flr.at[stage, at],
                                            device_id=(me, to), device_id_type=MESH)

    def told(stage, i):
        ref, at, to = ((flx, sx, x_peer(i)), (flz, sz, z_peer(i)))[stage]
        at = lax.rem(at + i, 4)
        return pltpu.make_async_remote_copy(ref.at[at], ref.at[at], fls.at[stage, i], flr.at[stage, at],
                                            device_id=(me, to), device_id_type=MESH)

    flx[sx] = jnp.broadcast_to(over, (8, COLS))
    for i in (1, 2, 3):
        tell(0, i).start()
    for w in weights:
        w.wait()

    def sources(j):
        def each(d, carry):
            arrival(j, d).wait_recv()
            return carry
        lax.fori_loop(0, PEERS, each, 0)

        def prepare(i, total):
            at = pl.ds(pl.multiple_of(i * LB, LB), LB)
            field = got[j, at, :]
            state[at, :] = field.astype(bf16)
            square[at, :] = (field * field).astype(bf16)
            return total + jnp.sum((bandb[at, :] * field).reshape(LB // 8, 8, COLS), axis=0)
        energy = jnp.sum(lax.fori_loop(0, PEERS, prepare, jnp.zeros((8, COLS), f32)), axis=0, keepdims=True)
        damp = 1.0 / (1.0 + 0.5 * energy)

        def owner(i, carry):
            d = lax.rem(me + i, PEERS)
            at = pl.ds(pl.multiple_of(d * LB, LB), LB)
            gain = jnp.dot(kgv[at, :], state[...], preferred_element_type=f32)
            loss = jnp.dot(klv[at, :], square[...], preferred_element_type=f32)
            field = got[j, at, :]
            fresh[j, at, :] = (field * (growb[at, :] + 0.25 * gain) - 0.25 * loss) * damp

            @pl.when(i < PEERS)
            def _():
                give(j, d).start()
            return carry
        lax.fori_loop(1, PEERS + 1, owner, 0)
        pltpu.make_async_copy(
            fresh.at[j, pl.ds(me * LB, LB), :], back.at[pl.ds(seat(8 * j + mine), LB), :], br.at[8 * j + mine]).start()

    def full_rounds(j, carry):
        sources(j)
        return carry
    lax.fori_loop(0, 6, full_rounds, 0)

    @pl.when(core == 0)
    def _():
        sources(6)

    for i in (1, 2, 3):
        told(0, i).wait_recv()
    flz[sz] = jnp.maximum(jnp.maximum(flx[0], flx[1]), jnp.maximum(flx[2], flx[3]))
    for i in (1, 2, 3):
        tell(1, i).start()

    for p, g in enumerate(ORDER):
        total[...] = jnp.zeros_like(total)

        def pull(i, carry):
            q = BASE * p + i
            returned(q).wait_recv()
            cells = back[pl.ds(pl.multiple_of((16 * p + i) * LB, LB), LB), :]
            high = cells.astype(bf16)
            low = (cells - high.astype(f32)).astype(bf16)
            both = jnp.concatenate([high, low], axis=0)
            total[...] += lax.dot_general(both, place[q], (((1,), (1,)), ((), ())), preferred_element_type=f32)
            return carry
        lax.fori_loop(0, BASE, pull, 0)
        for k in range(EXT):
            at = slice(k * COLS, (k + 1) * COLS)
            back[pl.ds((16 * p + BASE + k) * LB, LB), :] = total[:LB, at] + total[LB:, at]
        for h in (0, 1):
            r0 = 16 * g + 8 * h
            sea = mask[r0:r0 + 8, :].astype(f32)

            def turn(b, carry):
                out[b, pl.ds(r0, 8), :] = back[pl.ds((16 * p + 8 * h) * LB + b, 8, stride=LB), :] * sea
                return carry
            lax.fori_loop(0, LB, turn, 0, unroll=8)

    for i in (1, 2, 3):
        told(1, i).wait_recv()
    flag[...] = jnp.maximum(jnp.maximum(flz[0], flz[1]), jnp.maximum(flz[2], flz[3]))
    for h in halos:
        h.wait_send()
    for i in (1, 2, 3):
        tell(0, i).wait_send()
        tell(1, i).wait_send()

    def drain(q, carry):
        d, copy = forward(q)

        @pl.when(d != me)
        def _():
            copy.wait_send()
        return carry
    lax.fori_loop(0, TILES, drain, 0)

    def drain_round(j):
        def step(i, carry):
            give(j, lax.rem(me + i, PEERS)).wait_send()
            return carry
        lax.fori_loop(1, PEERS, step, 0)

    for j in range(6):
        drain_round(j)

    @pl.when(core == 0)
    def _():
        drain_round(6)


def finish_kernel(packed, out, sems):
    part = LB // 8
    copies = [pltpu.make_async_copy(packed.at[pl.ds(i * part, part)], out.at[pl.ds(i * part, part)], sems.at[i]) for i in range(8)]
    for copy in copies:
        copy.start()
    for copy in copies:
        copy.wait()


def local(spectra, land_mask, growth, band_weight, kernel_gain, kernel_loss):
    theta = 2.0 * math.pi * (np.arange(LB) % ND + 0.5) / ND
    wide = lambda v: jnp.asarray(np.repeat(v.astype(np.float32)[:, None], COLS, 1))
    vmem = pl.BlockSpec(memory_space=pltpu.VMEM)
    anym = pl.BlockSpec(memory_space=pl.ANY)
    f32, bf16, i32 = jnp.float32, jnp.bfloat16, jnp.int32
    dma = pltpu.SemaphoreType.DMA
    shape = jax.ShapeDtypeStruct((LB, ROWS, COLS), f32)
    operands = (spectra, land_mask, wide(np.cos(theta)), wide(np.sin(theta)),
                growth.reshape(NB // COLS, COLS), band_weight.reshape(NB // COLS, COLS), kernel_gain, kernel_loss)
    in_specs = [anym, vmem, vmem, vmem, vmem, vmem, anym, anym]
    weights = [
        pltpu.VMEM((NB, NB), bf16),
        pltpu.VMEM((NB, NB), bf16),
        pltpu.VMEM((NB, COLS), f32),
        pltpu.VMEM((NB, COLS), f32),
        pltpu.VMEM((NB, COLS), bf16),
        pltpu.VMEM((NB, COLS), bf16),
    ]
    edges = [
        pltpu.VMEM((LB, PAD, COLS), f32),
        pltpu.VMEM((PAD, 8, COLS), f32),
        pltpu.VMEM((8, COLS), i32),
        pltpu.VMEM((8, COLS), i32),
    ]

    def finish(packed):
        return pl.pallas_call(
            finish_kernel,
            out_shape=shape,
            in_specs=[vmem],
            out_specs=anym,
            scratch_shapes=[dma((8,))],
            compiler_params=pltpu.CompilerParams(vmem_limit_bytes=16 * 2**20),
        )(packed)

    def whole(args):
        return (pl.pallas_call(
            whole_kernel,
            out_shape=pltpu.VMEM((LB, ROWS, COLS), f32),
            in_specs=in_specs,
            out_specs=vmem,
            scratch_shapes=edges + [
                pltpu.VMEM((ROWS, LB, COLS), f32),
                pltpu.VMEM((ROUNDS, NB, COLS), f32),
                pltpu.VMEM((ROUNDS, NB, COLS), f32),
                pltpu.VMEM((ROWS * LB, COLS), f32),
            ] + weights + [
                dma((10,)), dma((4,)), dma((4,)), dma((2, ROUNDS)),
                dma((ROUNDS, PEERS)), dma((ROUNDS, PEERS)), dma((ROUNDS, PEERS)), dma((ROUNDS, PEERS)),
            ],
            compiler_params=pltpu.CompilerParams(collective_id=1, has_side_effects=True, vmem_limit_bytes=58 * 2**20),
        )(*args[1:]))

    packed, flag = pl.pallas_call(
        sea_kernel,
        out_shape=(pltpu.VMEM((LB, ROWS, COLS), f32), pltpu.VMEM((8, COLS), f32)),
        in_specs=[anym] * 8,
        out_specs=(vmem, vmem),
        scratch_shapes=edges + [
            pltpu.VMEM((TILES, LB, COLS), f32),
            pltpu.VMEM((EXT, LB, COLS), f32),
            pltpu.VMEM((2 * LB, EXT * COLS), bf16),
            pltpu.VMEM((TILES, EXT * COLS, COLS), bf16),
            pltpu.VMEM((16, COLS), f32),
            pltpu.VMEM((7, NB, COLS), f32),
            pltpu.VMEM((7, NB, COLS), f32),
            pltpu.VMEM((ROWS * LB, COLS), f32),
            pltpu.VMEM((2 * LB, EXT * COLS), f32),
        ] + weights + [
            pltpu.VMEM((4, 8, COLS), f32),
            pltpu.VMEM((4, 8, COLS), f32),
            dma((10,)), dma((4,)), dma((4,)),
            dma((TILES,)), dma((7, PEERS)), dma((7, PEERS)), dma((TILES,)),
            dma((2, 4)), dma((2, 4)), dma((8,)),
            pltpu.VMEM((ROWS, COLS), i32),
            pltpu.VMEM((LB, COLS), f32),
            pltpu.VMEM((LB, COLS), f32),
            pltpu.VMEM((NB // COLS, COLS), f32),
            pltpu.VMEM((NB // COLS, COLS), f32),
            dma((5,)),
        ],
        compiler_params=pltpu.CompilerParams(collective_id=0, has_side_effects=True, vmem_limit_bytes=58 * 2**20),
    )(*operands)
    return lax.cond(flag[0, 0] > 0.0, whole, lambda args: args[0], (packed,) + operands)


def solution(mesh):
    in_specs = (P("bins", "space", None), P("space", None), P(), P(), P(), P())
    out_specs = P("bins", "space", None)
    return jax.shard_map(local, mesh=mesh, in_specs=in_specs, out_specs=out_specs, check_vma=False)
```
